512 devices in a mesh: dp: 32 (over x, y), expert: 16 (over z, core).
Axes of the slice: x: 4, y: 8, z: 8, core: 2. Of those that a mesh axis runs over, the one named last changes fastest.
Arguments:
- tokens: bfloat16 [65536, 1792], P(('dp', 'expert')), may hold values from -6 to 6
- routes: int32 [65536, 2], P(('dp', 'expert')), may hold values from 0 to 15, all different within a row; in each aligned block of 128 rows (0 to 127, 128 to 255, ...) at most 32 rows name the same one
- gates: float32 [65536, 2], P(('dp', 'expert')), may hold values from 0.25 to 1
- grad_hidden: bfloat16 [65536, 2, 512], P(('dp', 'expert')), may hold values from -4 to 4
- w_in: bfloat16 [16, 1792, 512], P('expert', 'dp'), may hold values from -0.25 to 0.25
- error: bfloat16 [32, 16, 1792, 512], P('dp', 'expert'), may hold values from -6 to 6
- q_seed: float32 [16, 512, 32], P('expert'), may hold values from -6 to 6
Outputs:
- grad_tokens: bfloat16 [65536, 1792], P(('dp', 'expert'))
- error_next: bfloat16 [32, 16, 1792, 512], P('dp', 'expert')
- weight_grad: float32 [16, 1792, 512], P('expert', 'dp')
The draws below stay inside these ranges and needn't reach their ends.
Inputs may be any that keep to these rules, and one draw needn't show every extreme that they name: `routes`: in the rows of one device no expert is named by more than 32 rows, a bound that some block reaches; the two experts of a row differ.
All inputs are finite; a program needn't handle non-finite values.
Results may differ from the reference program's by a relative error of at most 0.014.
Values may be sent and summed in bfloat16 or wider, within the bound.
No kernel may reach another device: no remote copies, remote signals or barrier semaphores. Data moves between devices by JAX's collectives and lax.ppermute only.
A program may use at most 64 MiB of HBM per device.

```python
import math
import jax
import jax.numpy as jnp
import numpy as np
from jax import lax

D = 1792
F = 512
RANK = 32
TOK_DEV = 128
EXPERTS = 16
REPLICAS = 32
CAP = 32
TOKENS = 65536
N_DP = 32
N_EXPERT = 16


def block_scale(own_key, dims, split, smallest, high):
    level, own = 1.0, jax.random.fold_in(own_key, 6)
    for position, blocks in split:
        draws = jnp.exp(jax.random.uniform(jax.random.fold_in(own, position), (blocks,), jnp.float32, smallest / len(split), high / len(split)))
        level = level * jnp.repeat(draws, dims[position] // blocks).reshape([-1 if axis == position else 1 for axis in range(len(dims))])
    return level


def shared_out(stream_key, own, number, rows, count, top, limit, lean):
    order = jax.random.permutation(stream_key, count)
    heavy_load, usual = portions_of(count, rows * top, limit, lean, True), portions_of(count, rows * top, limit, lean, False)
    places = jnp.arange(count)

    def named(lengths, turn):
        used = int((lengths > 0).sum())
        fixed = max(1, used // 4)
        shifted = fixed + (places - fixed + turn * (used - fixed)) % max(1, count - fixed)
        return jnp.zeros((count,), jnp.int32).at[order[jnp.where(places < fixed, places, shifted)]].set(jnp.asarray(lengths, jnp.int32))

    lengths = jnp.where(number % 4 == 0, named(heavy_load, number // 4), named(usual, number - number // 4 - 1))
    mixed = jax.random.permutation(jax.random.fold_in(own, 3), count)
    source_of, sink = mixed[0:count // 2 * 2:2], mixed[1:count // 2 * 2:2]
    slack = jnp.minimum(lengths[source_of] - 1, limit - lengths[sink]) // 2
    slack = jnp.where((source_of == order[0]) | (sink == order[0]) | (lengths[sink] == 0), 0, jnp.maximum(slack, 0))
    shifted = jax.random.randint(jax.random.fold_in(own, 4), (count // 2,), 0, 1 << 20) % (slack + 1)
    lengths = lengths.at[source_of].add(-shifted).at[sink].add(shifted)
    members = jnp.searchsorted(jnp.cumsum(lengths), jnp.arange(rows * top), side="right").astype(jnp.int32)
    listing = members.reshape(top, rows).T
    listing = listing[jax.random.permutation(jax.random.fold_in(own, 1), rows)]
    turn = jax.random.randint(jax.random.fold_in(own, 2), (rows, 1), 0, top)
    return jnp.take_along_axis(listing, (jnp.arange(top)[None, :] + turn) % top, axis=1)


def portions_of(count, total, limit, lean, full):
    weights = [(1 << 20) // math.isqrt(rank ** lean) + 1 for rank in range(1, count + 1)]
    largest = limit if full else min(limit, max(-(-total // count), total * weights[0] // sum(weights)))
    least = 1 if total - largest >= count - 1 else 0
    holding, spare = [largest] + [least] * (count - 1), total - largest - least * (count - 1)
    while spare > 0:
        movable = [i for i in range(1, count) if holding[i] < largest] or [i for i in range(1, count) if holding[i] < limit]
        mass, budget = sum([weights[i] for i in movable]), spare
        for i in movable:
            more = min(limit - holding[i], max(1, budget * weights[i] // mass), spare)
            holding[i] = holding[i] + more
            spare = spare - more
    return np.array(holding)


def gaussian(rng, extent, scale, bound, pieces=(), kind=jnp.bfloat16):
    values = jax.random.normal(rng, extent, jnp.float32) * scale
    if len(pieces) > 0:
        values = block_scale(rng, extent, pieces, -0.22, 0.18) * values
    return jnp.clip(values, min=-bound, max=bound).astype(kind)


def setup_inputs(seed: int = 0) -> dict:
    arg_keys = jax.random.split(jax.random.key(seed), 8)
    tokens = gaussian(arg_keys[0], (TOKENS, D), 1.0, 6.0, ((0, 512),))
    routes_keys = jax.random.split(jax.random.fold_in(arg_keys[1], 1), TOKENS // TOK_DEV)
    routes_turns = jax.random.permutation(jax.random.fold_in(arg_keys[1], 3), TOKENS // TOK_DEV)
    routes = jax.vmap(lambda own, number: shared_out(jax.random.fold_in(arg_keys[1], 2), own, number, TOK_DEV, EXPERTS, 2, CAP, 1))(routes_keys, routes_turns).reshape((TOKENS, 2))
    gates = jnp.clip(0.25 + 0.75 * jax.random.uniform(arg_keys[2], (TOKENS, 2), jnp.float32) ** block_scale(arg_keys[2], (TOKENS, 2), ((0, 512),), -0.2, 0.2), 0.25, 1.0)
    grad_hidden = gaussian(arg_keys[3], (TOKENS, 2, F), 0.5, 4.0, ((0, 512),))
    w_in = gaussian(arg_keys[4], (EXPERTS, D, F), F ** -0.5, 0.25, ((0, 16), (1, 32)))
    error = gaussian(arg_keys[5], (REPLICAS, EXPERTS, D, F), 1.0, 6.0, ((0, 32), (1, 16)))
    q_seed = gaussian(arg_keys[6], (EXPERTS, F, RANK), 1.0, 6.0, ((0, 16),), jnp.float32)
    return dict(tokens=tokens, routes=routes, gates=gates, grad_hidden=grad_hidden, w_in=w_in, error=error, q_seed=q_seed)


highest = lax.Precision.HIGHEST

def slopes(pre_act):
    squashed = jax.nn.sigmoid(pre_act)
    return squashed * (1.0 + pre_act * (1.0 - squashed))

def gram_schmidt(factor):
    height = factor.shape[0]

    def column(ordinal, basis):
        vector = lax.dynamic_index_in_dim(basis, ordinal, 0, keepdims=False)
        vector = vector / jnp.sqrt(jnp.sum(vector * vector))
        coeffs = jnp.dot(basis, vector, precision=highest)
        beyond = (jnp.arange(height) > ordinal).astype(basis.dtype)
        basis = basis - (coeffs * beyond)[:, None] * vector[None, :]
        return lax.dynamic_update_index_in_dim(basis, vector, ordinal, 0)
    return lax.fori_loop(0, height, column, factor)

def choose_slots(chosen, expert):
    matches = chosen == expert
    slots = jnp.cumsum(matches.astype(jnp.int32)) - 1
    target = jnp.where(matches, slots, CAP).astype(jnp.int32)
    ordinal = jnp.arange(chosen.shape[0], dtype=jnp.int32)
    indices = jnp.zeros((CAP + 1,), jnp.int32).at[target].set(ordinal)[:CAP]
    filled = jnp.zeros((CAP + 1,), jnp.float32).at[target].set(1.0)[:CAP]
    return (indices, filled)

def take_rows(source, places):
    return source[places]

def add_rows(buffer, places, values):
    return buffer.at[places].add(values)

def replica_work(arrived, arrived_grad, stored, weight):
    pre_act = jnp.dot(arrived, weight, preferred_element_type=jnp.float32)
    grad_pre = (arrived_grad.astype(jnp.float32) * slopes(pre_act)).astype(jnp.bfloat16)
    weight_term = lax.dot_general(arrived, grad_pre, (((0,), (0,)), ((), ())), preferred_element_type=jnp.float32)
    grad_rows = lax.dot_general(grad_pre, weight, (((1,), (1,)), ((), ())), preferred_element_type=jnp.float32)
    return (weight_term + stored.astype(jnp.float32), grad_rows.astype(jnp.bfloat16))

def reference(tokens, routes, gates, grad_hidden, w_in, error, q_seed):
    blocks = tokens.reshape(N_DP, N_EXPERT, TOK_DEV, D)
    chosen_all = routes.reshape(N_DP, N_EXPERT, 2 * TOK_DEV)
    gate_all = gates.reshape(N_DP, N_EXPERT, 2 * TOK_DEV)
    grad_all = grad_hidden.reshape(N_DP, N_EXPERT, 2 * TOK_DEV, F)
    slot_finder = jax.vmap(jax.vmap(choose_slots, (0, None)), (0, None))
    take_twice = jax.vmap(jax.vmap(take_rows))
    add_twice = jax.vmap(jax.vmap(add_rows))
    work_all = jax.vmap(replica_work, (0, 0, 0, None))

    def per_expert(running, expert):
        indices, filled = slot_finder(chosen_all, expert)
        token_rows = indices // 2
        gate_sel = take_twice(gate_all, indices) * filled
        scaled = (take_twice(blocks, token_rows).astype(jnp.float32) * gate_sel[..., None]).astype(jnp.bfloat16)
        sent_grad = (take_twice(grad_all, indices).astype(jnp.float32) * filled[..., None]).astype(jnp.bfloat16)
        weight = w_in[expert]
        merged, grad_rows = work_all(scaled.reshape(N_DP, N_EXPERT * CAP, D), sent_grad.reshape(N_DP, N_EXPERT * CAP, F), error[:, expert], weight)
        q_start = q_seed[expert].astype(jnp.float32)
        summed = jnp.einsum('fr,ndf->rd', q_start, merged, precision=highest) / N_DP
        basis = gram_schmidt(summed)
        q_factor = jnp.einsum('rd,ndf->rf', basis, merged, precision=highest) / N_DP
        low_rank = jnp.dot(basis.T, q_factor, precision=highest)
        error_out = (merged - low_rank[None]).astype(jnp.bfloat16)
        returned = grad_rows.reshape(N_DP, N_EXPERT, CAP, D).astype(jnp.float32) * gate_sel[..., None]
        running = add_twice(running, token_rows, returned)
        return (running, (error_out, low_rank))
    initial = jnp.zeros((N_DP, N_EXPERT, TOK_DEV, D), jnp.float32)
    running, (errors, low_rank) = lax.scan(per_expert, initial, jnp.arange(EXPERTS))
    grad_tokens = running.reshape(N_DP * N_EXPERT * TOK_DEV, D).astype(jnp.bfloat16)
    return (grad_tokens, jnp.transpose(errors, (1, 0, 2, 3)), low_rank)
```

```python
import jax
import jax.numpy as jnp
from jax import lax
from jax.experimental import pallas as pl
from jax.experimental.pallas import tpu as pltpu
from jax.sharding import Mesh
from jax.sharding import PartitionSpec as P

DP = ("dp_0", "dp_1")
DP_EXPERT = ("dp_0", "dp_1", "expert")

f32, bf16 = jnp.float32, jnp.bfloat16
VMEM = pl.BlockSpec(memory_space=pltpu.VMEM)
LANES = 128


def nn(a, b):
    return lax.dot_general(a, b, (((1,), (0,)), ((), ())), preferred_element_type=f32)


def nt(a, b):
    return lax.dot_general(a, b, (((1,), (1,)), ((), ())), preferred_element_type=f32)


def tn(a, b):
    return lax.dot_general(a, b, (((0,), (0,)), ((), ())), preferred_element_type=f32)


def halves(x):
    high = x.astype(bf16)
    return high, (x - high.astype(f32)).astype(bf16)


def call(kernel, outs, args, flops=0, moved=0, megabytes=28, **more):
    return pl.pallas_call(
        kernel,
        out_shape=outs,
        compiler_params=pltpu.CompilerParams(vmem_limit_bytes=megabytes << 20),
        cost_estimate=pl.CostEstimate(flops=flops, bytes_accessed=moved, transcendentals=0),
        **more,
    )(*args)


def one_hots(routes, experts, capacity):
    rows = routes.shape[1]
    slots = experts * capacity
    before = (
        lax.broadcasted_iota(jnp.int32, (rows, rows), 0) < lax.broadcasted_iota(jnp.int32, (rows, rows), 1)
    ).astype(bf16)
    expert = lax.broadcasted_iota(jnp.int32, (experts, rows), 0)
    slot = lax.broadcasted_iota(jnp.int32, (slots, rows), 0)
    started = jnp.zeros((experts, 1), f32)
    out = []
    for k in range(2):
        chosen = routes[k : k + 1, :]
        match = (expert == chosen).astype(f32)
        earlier = nn(match.astype(bf16), before) + started
        place = jnp.sum(match * earlier, axis=0, keepdims=True).astype(jnp.int32) + chosen * capacity
        out.append((slot == place).astype(f32))
        started = started + jnp.sum(match, axis=1, keepdims=True)
    return out


def prepare_kernel(experts, capacity, routes_ref, gates_ref, tokens_ref, grad_ref, sent_ref):
    width = tokens_ref.shape[1]
    hidden = grad_ref.shape[1] // 2
    first, second = one_hots(routes_ref[...], experts, capacity)
    gates = gates_ref[...]
    gate = jnp.sum(first * gates[0:1, :] + second * gates[1:2, :], axis=1, keepdims=True)
    either = (first + second).astype(bf16)
    sent_ref[:, :width] = (nn(either, tokens_ref[...]) * gate).astype(bf16)
    grads = nn(first.astype(bf16), grad_ref[:, :hidden]) + nn(second.astype(bf16), grad_ref[:, hidden:])
    sent_ref[:, width:] = grads.astype(bf16)


def select_kernel(experts, capacity, routes_ref, select_ref):
    rows = routes_ref.shape[1]
    for k, places in enumerate(one_hots(routes_ref[...], experts, capacity)):
        select_ref[k * rows : (k + 1) * rows, :] = places.T.astype(bf16)


def merge_kernel(
    width, arrived_ref, weight_ref, error_ref, seed_ref, grad_pre_ref, merged_ref, factor_ref
):
    rank = seed_ref.shape[1]
    pre = nn(arrived_ref[:, :width], weight_ref[...])
    s = 1.0 / (1.0 + jnp.exp(-pre))
    grad_pre = (arrived_ref[:, width:].astype(f32) * (s * (1.0 + pre * (1.0 - s)))).astype(bf16)
    grad_pre_ref[...] = grad_pre
    high, low = halves(seed_ref[...])
    both = jnp.concatenate([high, low], axis=1)
    step = width // 7
    for i in range(7):
        rows = slice(i * step, (i + 1) * step)
        merged = tn(arrived_ref[:, rows], grad_pre) + error_ref[rows, :].astype(f32)
        merged_ref[rows, :] = merged
        upper, lower = halves(merged)
        part = nn(upper, both)
        part = part[:, :rank] + part[:, rank:] + nn(lower, high)
        part = part.T
        for j in range(step // LANES):
            factor_ref[:, i * (step // LANES) + j, :] = part[:, j * LANES : (j + 1) * LANES]


def rows_kernel(grad_pre_ref, weight_ref, grad_rows_ref):
    grad_rows_ref[...] = nt(grad_pre_ref[...], weight_ref[...]).astype(bf16)


def sum_and_copy_kernel(parts_ref, copies_ref):
    total = jnp.sum(parts_ref[...], axis=0)
    copies_ref[...] = jnp.broadcast_to(total[None], copies_ref.shape)


def right_kernel(factor_ref, merged_ref, right_ref):
    rank, blocks, _ = factor_ref.shape
    total = jnp.zeros(right_ref.shape, f32)
    for j in range(0, blocks, 2):
        pair = jnp.concatenate([factor_ref[:, j, :], factor_ref[:, j + 1, :]], axis=1)
        both = jnp.concatenate(halves(pair), axis=0)
        part = nn(both, merged_ref[j * LANES : (j + 2) * LANES, :].astype(bf16))
        total = total + part[:rank] + part[rank:]
    right_ref[...] = total


def left_kernel(factor_ref, left_ref, gathered_ref):
    rank, blocks, _ = factor_ref.shape
    for j in range(blocks):
        gathered_ref[:, j * LANES : (j + 1) * LANES] = factor_ref[:, j, :]
    factor = gathered_ref[...]
    high, low = halves(factor)
    gram = nt(high, high) + nt(high, low) + nt(low, high)
    line = lax.broadcasted_iota(jnp.int32, (rank, rank), 0)
    column = lax.broadcasted_iota(jnp.int32, (rank, rank), 1)
    eye = (line == column).astype(f32)

    def eliminate(i, both):
        gram, inverse = both
        own = line == i
        at_column = jnp.where(column == i, gram, 0.0)
        entries = jnp.sum(at_column, axis=1, keepdims=True)
        pivot = jnp.sum(jnp.where(own, at_column, 0.0), axis=(0, 1), keepdims=True)
        row = jnp.sum(jnp.where(own, gram, 0.0), axis=0, keepdims=True) / pivot
        inverse_row = jnp.sum(jnp.where(own, inverse, 0.0), axis=0, keepdims=True) / pivot
        return (
            jnp.where(own, row, gram - entries * row),
            jnp.where(own, inverse_row, inverse - entries * inverse_row),
        )

    _, inverse = lax.fori_loop(0, rank, eliminate, (gram, eye))
    upper, lower = halves(inverse)
    left_ref[...] = nn(upper, high) + nn(upper, low) + nn(lower, high)


def finish_kernel(count, total_ref, left_ref, mine_ref, merged_ref, error_ref, weight_ref, right_ref):
    @pl.when(pl.program_id(0) == 0)
    def _():
        total = total_ref[...] / count
        high, low = halves(total)
        right_ref[...] = jnp.concatenate([high, low, high], axis=0)
        upper, lower = halves(mine_ref[...])
        weight_ref[...] = tn(jnp.concatenate([upper, upper, lower], axis=0), right_ref[...])

    upper, lower = halves(left_ref[...])
    low_rank = tn(jnp.concatenate([upper, upper, lower], axis=0), right_ref[...])
    error_ref[...] = (merged_ref[...] - low_rank).astype(bf16)


def combine_kernel(select_ref, gates_ref, returned_ref, out_ref):
    rows = out_ref.shape[0]
    returned = returned_ref[...]
    picked = nn(select_ref[...], returned)
    gates = gates_ref[...]
    out_ref[...] = (picked[:rows] * gates[:, 0:1] + picked[rows:] * gates[:, 1:2]).astype(bf16)


def shape(dims, dtype):
    return jax.ShapeDtypeStruct(dims, dtype)


def summed(x, axis):
    size, step = lax.axis_size(axis), 1
    while step < size:
        x = x + lax.ppermute(x, axis, [(i, i ^ step) for i in range(size)])
        step *= 2
    return x


def body(tokens, routes, gates, grad_hidden, w_in, error, q_seed):
    experts = lax.axis_size("expert")
    replicas = lax.axis_size(DP)
    row_count, width = tokens.shape
    hidden = grad_hidden.shape[2]
    rank = q_seed.shape[2]
    capacity = 4 * row_count // experts
    slots = experts * capacity
    routes_t = routes.T

    sent = call(
        lambda *refs: prepare_kernel(experts, capacity, *refs),
        shape((slots, width + hidden), bf16),
        (routes_t, gates.T, tokens, grad_hidden.reshape(row_count, 2 * hidden)),
    )
    w_mine, sent = lax.optimization_barrier((w_in[0], sent))
    arrived = lax.all_to_all(
        sent.reshape(experts, capacity, width + hidden), "expert", 0, 0, tiled=True
    ).reshape(slots, width + hidden)
    weight = lax.all_gather(lax.all_gather(w_mine, DP[1], tiled=True), DP[0], tiled=True)
    select = call(
        lambda *refs: select_kernel(experts, capacity, *refs),
        shape((2 * row_count, slots), bf16),
        (routes_t,),
    )

    blocks = width // LANES
    grad_pre, merged, factor = call(
        lambda *refs: merge_kernel(width, *refs),
        (shape((slots, hidden), bf16), shape((width, hidden), f32), shape((rank, blocks, LANES), f32)),
        (arrived, weight, error[0, 0], q_seed[0]),
    )
    each = rank // replicas
    parts = lax.all_to_all(factor, DP, 0, 0, tiled=True)
    grad_rows = call(rows_kernel, shape((slots, width), bf16), (grad_pre, weight))
    copies = call(
        sum_and_copy_kernel,
        shape((replicas, each * blocks, LANES), f32),
        (parts.reshape(replicas, each * blocks, LANES),),
    )
    factor = lax.all_to_all(copies, DP, 0, 0, tiled=True).reshape(rank, blocks, LANES)
    factor, grad_rows = lax.optimization_barrier((factor, grad_rows))
    returned = lax.all_to_all(
        grad_rows.reshape(experts, capacity, width), "expert", 0, 0, tiled=True
    ).reshape(slots, width)

    right = call(right_kernel, shape((rank, hidden), f32), (factor, merged))
    right = summed(summed(right, DP[1]), DP[0])
    left = call(
        left_kernel,
        shape((rank, width), f32),
        (factor,),
        scratch_shapes=[pltpu.VMEM((rank, width), f32)],
    )
    shard = width // replicas
    mine = lax.dynamic_slice_in_dim(left, lax.axis_index(DP) * shard, shard, 1)

    step = width // 7
    error_next, weight_grad = call(
        lambda *refs: finish_kernel(replicas, *refs),
        (shape((width, hidden), bf16), shape((shard, hidden), f32)),
        (right, left, mine, merged),
        grid=(7,),
        in_specs=[
            pl.BlockSpec((rank, hidden), lambda i: (0, 0)),
            pl.BlockSpec((rank, step), lambda i: (0, i)),
            pl.BlockSpec((rank, shard), lambda i: (0, 0)),
            pl.BlockSpec((step, hidden), lambda i: (i, 0)),
        ],
        out_specs=[
            pl.BlockSpec((step, hidden), lambda i: (i, 0)),
            pl.BlockSpec((shard, hidden), lambda i: (0, 0)),
        ],
        scratch_shapes=[pltpu.VMEM((3 * rank, hidden), bf16)],
    )
    grad_tokens = call(combine_kernel, shape((row_count, width), bf16), (select, gates, returned))
    return grad_tokens, error_next[None, None], weight_grad[None]


def solution(mesh):
    torus = Mesh(mesh.devices.reshape(4, 8, mesh.shape["expert"]), DP_EXPERT)
    in_specs = (
        P(DP_EXPERT, None),
        P(DP_EXPERT, None),
        P(DP_EXPERT, None),
        P(DP_EXPERT, None, None),
        P("expert", DP, None),
        P(DP, "expert", None, None),
        P("expert", None, None),
    )
    out_specs = (P(DP_EXPERT, None), P(DP, "expert", None, None), P("expert", DP, None))
    return jax.shard_map(body, mesh=torus, in_specs=in_specs, out_specs=out_specs, check_vma=False)
```

```python
import jax
import jax.numpy as jnp
from jax import lax
from jax.experimental import pallas as pl
from jax.experimental.pallas import tpu as pltpu
from jax.sharding import Mesh
from jax.sharding import PartitionSpec as P

DP = ("dp_0", "dp_1")
DP_EXPERT = ("dp_0", "dp_1", "expert")

f32, bf16 = jnp.float32, jnp.bfloat16
HBM = pl.BlockSpec(memory_space=pltpu.HBM)
VMEM = pl.BlockSpec(memory_space=pltpu.VMEM)
TILES = 7
ROOM = 50_000_000
LANES = 128


def nn(a, b):
    return lax.dot_general(a, b, (((1,), (0,)), ((), ())), preferred_element_type=f32)


def nt(a, b):
    return lax.dot_general(a, b, (((1,), (1,)), ((), ())), preferred_element_type=f32)


def tn(a, b):
    return lax.dot_general(a, b, (((0,), (0,)), ((), ())), preferred_element_type=f32)


def halves(x):
    high = x.astype(bf16)
    return high, (x - high.astype(f32)).astype(bf16)


def call(kernel, outs, args, room=63_400_000, **more):
    return pl.pallas_call(
        kernel,
        out_shape=outs,
        compiler_params=pltpu.CompilerParams(vmem_limit_bytes=room),
        cost_estimate=pl.CostEstimate(flops=0, bytes_accessed=0, transcendentals=0),
        **more,
    )(*args)


def one_hots(routes, experts, capacity):
    rows = routes.shape[1]
    slots = experts * capacity
    before = (
        lax.broadcasted_iota(jnp.int32, (rows, rows), 0) < lax.broadcasted_iota(jnp.int32, (rows, rows), 1)
    ).astype(bf16)
    expert = lax.broadcasted_iota(jnp.int32, (experts, rows), 0)
    slot = lax.broadcasted_iota(jnp.int32, (slots, rows), 0)
    started = jnp.zeros((experts, 1), f32)
    out = []
    for k in range(2):
        chosen = routes[k : k + 1, :]
        match = (expert == chosen).astype(f32)
        earlier = nn(match.astype(bf16), before) + started
        place = jnp.sum(match * earlier, axis=0, keepdims=True).astype(jnp.int32) + chosen * capacity
        out.append((slot == place).astype(f32))
        started = started + jnp.sum(match, axis=1, keepdims=True)
    return out


def prepare_kernel(
    experts, capacity, routes_hbm, gates_hbm, tokens_hbm, grad_hbm, sent_hbm, routes, gates, tokens, grad, sent, sem
):
    width = tokens.shape[1]
    hidden = grad.shape[1] // 2
    copies = [
        pltpu.make_async_copy(routes_hbm, routes, sem.at[0]),
        pltpu.make_async_copy(gates_hbm, gates, sem.at[1]),
        pltpu.make_async_copy(tokens_hbm, tokens, sem.at[2]),
        pltpu.make_async_copy(grad_hbm, grad, sem.at[3]),
    ]
    for copy in copies:
        copy.start()
    copies[0].wait()
    first, second = one_hots(routes[...], experts, capacity)
    copies[1].wait()
    gate = jnp.sum(first * gates[0:1, :] + second * gates[1:2, :], axis=1, keepdims=True)
    either, first, second = (first + second).astype(bf16), first.astype(bf16), second.astype(bf16)
    copies[2].wait()
    copies[3].wait()
    parts = 4
    step = first.shape[0] // parts
    done = []
    for i in range(parts):
        rows = slice(i * step, (i + 1) * step)
        sent[rows, :width] = (nn(either[rows], tokens[...]) * gate[rows]).astype(bf16)
        grads = nn(first[rows], grad[:, :hidden]) + nn(second[rows], grad[:, hidden:])
        sent[rows, width:] = grads.astype(bf16)
        copy = pltpu.make_async_copy(sent.at[rows], sent_hbm.at[rows], sem.at[4 + i])
        copy.start()
        done.append(copy)
    for copy in done:
        copy.wait()


def select_kernel(experts, capacity, routes_ref, select_ref):
    rows = routes_ref.shape[1]
    for k, places in enumerate(one_hots(routes_ref[...], experts, capacity)):
        select_ref[k * rows : (k + 1) * rows, :] = places.T.astype(bf16)


def merge_kernel(
    width,
    arrived_hbm,
    weight_0_hbm,
    weight_1_hbm,
    error_hbm,
    seed_ref,
    grad_pre_ref,
    merged_hbm,
    rounded_hbm,
    factor_ref,
    arrived_ref,
    weight_0,
    weight_1,
    error,
    merged,
    rounded,
    arrived_sem,
    weight_sem,
    error_sem,
    merged_sem,
    rounded_sem,
):
    rank = seed_ref.shape[1]
    step = width // TILES
    tiles = [slice(i * step, (i + 1) * step) for i in range(TILES)]
    needs = []
    for i, rows in enumerate(tiles):
        needs.append(
            [
                pltpu.make_async_copy(arrived_hbm.at[:, rows], arrived_ref.at[:, rows], arrived_sem.at[i]),
                pltpu.make_async_copy(weight_0_hbm.at[rows], weight_0.at[rows], weight_sem.at[2 * i]),
                pltpu.make_async_copy(weight_1_hbm.at[rows], weight_1.at[rows], weight_sem.at[2 * i + 1]),
            ]
        )
        for load in needs[i]:
            load.start()
    rest = slice(width, arrived_ref.shape[1])
    grads = pltpu.make_async_copy(arrived_hbm.at[:, rest], arrived_ref.at[:, rest], arrived_sem.at[TILES])
    grads.start()
    loads = [
        pltpu.make_async_copy(error_hbm.at[rows], error.at[rows], error_sem.at[i])
        for i, rows in enumerate(tiles)
    ]
    for load in loads:
        load.start()
    pre = jnp.zeros(grad_pre_ref.shape, f32)
    for i, rows in enumerate(tiles):
        for load in needs[i]:
            load.wait()
        weight = jnp.concatenate([weight_0[rows, :], weight_1[rows, :]], axis=1)
        pre = pre + nn(arrived_ref[:, rows], weight)
    grads.wait()
    s = 1.0 / (1.0 + jnp.exp(-pre))
    grad_pre = (arrived_ref[:, width:].astype(f32) * (s * (1.0 + pre * (1.0 - s)))).astype(bf16)
    grad_pre_ref[...] = grad_pre
    high, low = halves(seed_ref[...])
    both = jnp.concatenate([high, low], axis=1)
    stores = []
    for i, rows in enumerate(tiles):
        loads[i].wait()
        total = tn(arrived_ref[:, rows], grad_pre) + error[rows, :].astype(f32)
        upper, lower = halves(total)
        merged[rows, :] = total
        rounded[rows, :] = upper
        stores.append(pltpu.make_async_copy(merged.at[rows], merged_hbm.at[rows], merged_sem.at[i]))
        stores.append(pltpu.make_async_copy(rounded.at[rows], rounded_hbm.at[rows], rounded_sem.at[i]))
        for store in stores[-2:]:
            store.start()
        part = nn(upper, both)
        part = part[:, :rank] + part[:, rank:] + nn(lower, high)
        part = part.T
        for j in range(step // LANES):
            factor_ref[:, i * (step // LANES) + j, :] = part[:, j * LANES : (j + 1) * LANES]
    for store in stores:
        store.wait()


def rows_kernel(grad_pre_ref, weight_0, weight_1, grad_rows_ref):
    half = weight_0.shape[1]
    rows = nt(grad_pre_ref[:, :half], weight_0[...]) + nt(grad_pre_ref[:, half:], weight_1[...])
    grad_rows_ref[...] = rows.astype(bf16)


def sum_and_copy_kernel(parts_ref, copies_ref):
    total = jnp.sum(parts_ref[...], axis=0)
    copies_ref[...] = jnp.broadcast_to(total[None], copies_ref.shape)


def right_kernel(factor_ref, rounded_hbm, right_ref, rounded, sem):
    rank, blocks, _ = factor_ref.shape
    step = 2 * LANES
    loads = []
    for i in range(blocks // 2):
        rows = slice(i * step, (i + 1) * step)
        loads.append(pltpu.make_async_copy(rounded_hbm.at[rows], rounded.at[rows], sem.at[i]))
        loads[i].start()
    total = jnp.zeros(right_ref.shape, f32)
    for i in range(blocks // 2):
        pair = jnp.concatenate([factor_ref[:, 2 * i, :], factor_ref[:, 2 * i + 1, :]], axis=1)
        both = jnp.concatenate(halves(pair), axis=0)
        loads[i].wait()
        part = nn(both, rounded[i * step : (i + 1) * step, :])
        total = total + part[:rank] + part[rank:]
    right_ref[...] = total


def left_kernel(factor_ref, left_ref, gathered_ref):
    rank, blocks, _ = factor_ref.shape
    for j in range(blocks):
        gathered_ref[:, j * LANES : (j + 1) * LANES] = factor_ref[:, j, :]
    high, low = halves(gathered_ref[...])
    gram = nt(high, high) + nt(high, low) + nt(low, high)
    line = lax.broadcasted_iota(jnp.int32, (rank, rank), 0)
    column = lax.broadcasted_iota(jnp.int32, (rank, rank), 1)
    both = jnp.concatenate([gram, (line == column).astype(f32)], axis=1)
    own = lax.broadcasted_iota(jnp.int32, both.shape, 0)
    for i in range(rank):
        row = both[i : i + 1, :] / both[i : i + 1, i : i + 1]
        both = jnp.where(own == i, row, both - both[:, i : i + 1] * row)
    upper, lower = halves(both[:, rank:])
    left_ref[...] = nn(upper, high) + nn(upper, low) + nn(lower, high)


def finish_kernel(
    count, total_ref, left_ref, mine_ref, merged_hbm, error_hbm, weight_ref, merged, error, load_sem, store_sem
):
    step = merged.shape[0] // TILES
    tiles = [slice(i * step, (i + 1) * step) for i in range(TILES)]
    loads = [
        pltpu.make_async_copy(merged_hbm.at[rows], merged.at[rows], load_sem.at[i])
        for i, rows in enumerate(tiles)
    ]
    for load in loads:
        load.start()
    high, low = halves(total_ref[...] / count)
    right = jnp.concatenate([high, low, high], axis=0)
    upper, lower = halves(mine_ref[...])
    weight_ref[...] = tn(jnp.concatenate([upper, upper, lower], axis=0), right)
    stores = []
    for i, rows in enumerate(tiles):
        upper, lower = halves(left_ref[:, rows])
        low_rank = tn(jnp.concatenate([upper, upper, lower], axis=0), right)
        loads[i].wait()
        error[rows, :] = (merged[rows, :] - low_rank).astype(bf16)
        stores.append(pltpu.make_async_copy(error.at[rows], error_hbm.at[rows], store_sem.at[i]))
        stores[i].start()
    for store in stores:
        store.wait()


def combine_kernel(select_ref, gates_ref, returned_ref, out_hbm, out, store_sem):
    rows, width = out.shape
    step = width // TILES
    tiles = [slice(i * step, (i + 1) * step) for i in range(TILES)]
    gates = gates_ref[...]
    stores = []
    for i, c in enumerate(tiles):
        picked = nn(select_ref[...], returned_ref[:, c])
        out[:, c] = (picked[:rows] * gates[:, 0:1] + picked[rows:] * gates[:, 1:2]).astype(bf16)
        stores.append(pltpu.make_async_copy(out.at[:, c], out_hbm.at[:, c], store_sem.at[i]))
        stores[i].start()
    for store in stores:
        store.wait()


def shape(dims, dtype):
    return jax.ShapeDtypeStruct(dims, dtype)


def summed(x, axis):
    size = lax.axis_size(axis)
    partners = [1 << k for k in range(size.bit_length() - 1)]
    if len(partners) > 1:
        partners[-1] = size - 1
    for partner in partners:
        x = x + lax.ppermute(x, axis, [(i, i ^ partner) for i in range(size)])
    return x


def body(tokens, routes, gates, grad_hidden, w_in, error, q_seed):
    experts = lax.axis_size("expert")
    replicas = lax.axis_size(DP)
    row_count, width = tokens.shape
    hidden = grad_hidden.shape[2]
    rank = q_seed.shape[2]
    capacity = 4 * row_count // experts
    slots = experts * capacity
    routes_t = routes.T
    dma = pltpu.SemaphoreType.DMA

    sent = call(
        lambda *refs: prepare_kernel(experts, capacity, *refs),
        shape((slots, width + hidden), bf16),
        (routes_t, gates.T, tokens, grad_hidden.reshape(row_count, 2 * hidden)),
        in_specs=[HBM, HBM, HBM, HBM],
        out_specs=HBM,
        scratch_shapes=[
            pltpu.VMEM((2, row_count), jnp.int32),
            pltpu.VMEM((2, row_count), f32),
            pltpu.VMEM((row_count, width), bf16),
            pltpu.VMEM((row_count, 2 * hidden), bf16),
            pltpu.VMEM((slots, width + hidden), bf16),
            dma((8,)),
        ],
    )
    w_mine, sent = lax.optimization_barrier((w_in[0], sent))
    arrived = lax.all_to_all(
        sent.reshape(experts, capacity, width + hidden), "expert", 0, 0, tiled=True
    ).reshape(slots, width + hidden)
    weight = lax.all_gather(w_mine, DP[1], tiled=True)
    half = hidden // 2
    weight_0 = lax.all_gather(weight[:, :half], DP[0], tiled=True)
    weight_1 = lax.all_gather(weight[:, half:], DP[0], tiled=True)
    select = call(
        lambda *refs: select_kernel(experts, capacity, *refs),
        shape((2 * row_count, slots), bf16),
        (routes_t,),
    )

    blocks = width // LANES
    grad_pre, merged, rounded, factor = call(
        lambda *refs: merge_kernel(width, *refs),
        (
            shape((slots, hidden), bf16),
            shape((width, hidden), f32),
            shape((width, hidden), bf16),
            shape((rank, blocks, LANES), f32),
        ),
        (arrived, weight_0, weight_1, error[0, 0], q_seed[0]),
        in_specs=[HBM, HBM, HBM, HBM, VMEM],
        out_specs=[VMEM, HBM, HBM, VMEM],
        scratch_shapes=[
            pltpu.VMEM((slots, width + hidden), bf16),
            pltpu.VMEM((width, half), bf16),
            pltpu.VMEM((width, half), bf16),
            pltpu.VMEM((width, hidden), bf16),
            pltpu.VMEM((width, hidden), f32),
            pltpu.VMEM((width, hidden), bf16),
            dma((TILES + 1,)),
            dma((2 * TILES,)),
            dma((TILES,)),
            dma((TILES,)),
            dma((TILES,)),
        ],
    )
    each = rank // replicas
    parts = lax.all_to_all(factor, DP, 0, 0, tiled=True)
    grad_rows = call(rows_kernel, shape((slots, width), bf16), (grad_pre, weight_0, weight_1))
    copies = call(
        sum_and_copy_kernel,
        shape((replicas, each * blocks, LANES), f32),
        (parts.reshape(replicas, each * blocks, LANES),),
    )
    factor = lax.all_to_all(copies, DP, 0, 0, tiled=True).reshape(rank, blocks, LANES)
    right = call(
        right_kernel,
        shape((rank, hidden), f32),
        (factor, rounded),
        in_specs=[VMEM, HBM],
        scratch_shapes=[pltpu.VMEM((width, hidden), bf16), dma((blocks // 2,))],
    )
    right, grad_rows = lax.optimization_barrier((right, grad_rows))
    returned = lax.all_to_all(
        grad_rows.reshape(experts, capacity, width), "expert", 0, 0, tiled=True
    ).reshape(slots, width)

    right = summed(summed(right, DP[1]), DP[0])
    left = call(
        left_kernel,
        shape((rank, width), f32),
        (factor,),
        scratch_shapes=[pltpu.VMEM((rank, width), f32)],
    )
    shard = width // replicas
    mine = lax.dynamic_slice_in_dim(left, lax.axis_index(DP) * shard, shard, 1)
    error_next, weight_grad = call(
        lambda *refs: finish_kernel(replicas, *refs),
        (shape((width, hidden), bf16), shape((shard, hidden), f32)),
        (right, left, mine, merged),
        in_specs=[VMEM, VMEM, VMEM, HBM],
        out_specs=[HBM, VMEM],
        scratch_shapes=[
            pltpu.VMEM((width, hidden), f32),
            pltpu.VMEM((width, hidden), bf16),
            dma((TILES,)),
            dma((TILES,)),
        ],
    )
    grad_tokens = call(
        combine_kernel,
        shape((row_count, width), bf16),
        (select, gates, returned),
        room=ROOM,
        in_specs=[VMEM, VMEM, VMEM],
        out_specs=HBM,
        scratch_shapes=[pltpu.VMEM((row_count, width), bf16), dma((TILES,))],
    )
    return grad_tokens, error_next[None, None], weight_grad[None]


def solution(mesh):
    torus = Mesh(mesh.devices.reshape(4, 8, mesh.shape["expert"]), DP_EXPERT)
    in_specs = (
        P(DP_EXPERT, None),
        P(DP_EXPERT, None),
        P(DP_EXPERT, None),
        P(DP_EXPERT, None, None),
        P("expert", DP, None),
        P(DP, "expert", None, None),
        P("expert", None, None),
    )
    out_specs = (P(DP_EXPERT, None), P(DP, "expert", None, None), P("expert", DP, None))
    return jax.shard_map(body, mesh=torus, in_specs=in_specs, out_specs=out_specs, check_vma=False)
```

```python
import jax
import jax.numpy as jnp
from jax import lax
from jax.experimental import pallas as pl
from jax.experimental.pallas import tpu as pltpu
from jax.sharding import Mesh
from jax.sharding import PartitionSpec as P

DP = ("dp_0", "dp_1")
DP_EXPERT = ("dp_0", "dp_1", "expert")

f32, bf16 = jnp.float32, jnp.bfloat16
HBM = pl.BlockSpec(memory_space=pltpu.HBM)
VMEM = pl.BlockSpec(memory_space=pltpu.VMEM)
TILES = 7
ROOM = 16_000_000
FULL = 63_400_000
LANES = 128


def nn(a, b):
    return lax.dot_general(a, b, (((1,), (0,)), ((), ())), preferred_element_type=f32)


def nt(a, b):
    return lax.dot_general(a, b, (((1,), (1,)), ((), ())), preferred_element_type=f32)


def tn(a, b):
    return lax.dot_general(a, b, (((0,), (0,)), ((), ())), preferred_element_type=f32)


def halves(x):
    high = x.astype(bf16)
    return high, (x - high.astype(f32)).astype(bf16)


def call(kernel, outs, args, room=ROOM, **more):
    return pl.pallas_call(
        kernel,
        out_shape=outs,
        compiler_params=pltpu.CompilerParams(vmem_limit_bytes=room),
        cost_estimate=pl.CostEstimate(flops=0, bytes_accessed=0, transcendentals=0),
        **more,
    )(*args)


def one_hots(routes, experts, capacity):
    rows = routes.shape[1]
    slots = experts * capacity
    before = (
        lax.broadcasted_iota(jnp.int32, (rows, rows), 0) < lax.broadcasted_iota(jnp.int32, (rows, rows), 1)
    ).astype(bf16)
    expert = lax.broadcasted_iota(jnp.int32, (experts, rows), 0)
    slot = lax.broadcasted_iota(jnp.int32, (slots, rows), 0)
    started = jnp.zeros((experts, 1), f32)
    out = []
    for k in range(2):
        chosen = routes[k : k + 1, :]
        match = (expert == chosen).astype(f32)
        earlier = nn(match.astype(bf16), before) + started
        place = jnp.sum(match * earlier, axis=0, keepdims=True).astype(jnp.int32) + chosen * capacity
        out.append((slot == place).astype(f32))
        started = started + jnp.sum(match, axis=1, keepdims=True)
    return out


def prepare_kernel(
    experts, capacity, routes_hbm, gates_hbm, tokens_hbm, grad_hbm, sent_hbm, routes, gates, tokens, grad, sent, sem
):
    width = tokens.shape[1]
    hidden = grad.shape[1] // 2
    copies = [
        pltpu.make_async_copy(routes_hbm, routes, sem.at[0]),
        pltpu.make_async_copy(gates_hbm, gates, sem.at[1]),
        pltpu.make_async_copy(tokens_hbm, tokens, sem.at[2]),
        pltpu.make_async_copy(grad_hbm, grad, sem.at[3]),
    ]
    for copy in copies:
        copy.start()
    copies[0].wait()
    first, second = one_hots(routes[...], experts, capacity)
    copies[1].wait()
    gate = jnp.sum(first * gates[0:1, :] + second * gates[1:2, :], axis=1, keepdims=True)
    either, first, second = (first + second).astype(bf16), first.astype(bf16), second.astype(bf16)
    copies[2].wait()
    copies[3].wait()
    parts = 4
    step = first.shape[0] // parts
    done = []
    for i in range(parts):
        rows = slice(i * step, (i + 1) * step)
        sent[rows, :width] = (nn(either[rows], tokens[...]) * gate[rows]).astype(bf16)
        grads = nn(first[rows], grad[:, :hidden]) + nn(second[rows], grad[:, hidden:])
        sent[rows, width:] = grads.astype(bf16)
        copy = pltpu.make_async_copy(sent.at[rows], sent_hbm.at[rows], sem.at[4 + i])
        copy.start()
        done.append(copy)
    for copy in done:
        copy.wait()


def select_kernel(experts, capacity, routes_ref, select_ref):
    rows = routes_ref.shape[1]
    for k, places in enumerate(one_hots(routes_ref[...], experts, capacity)):
        select_ref[k * rows : (k + 1) * rows, :] = places.T.astype(bf16)


def merge_kernel(
    width, arrived_ref, weight_0, weight_hbm, error_hbm, seed_ref, grad_pre_ref, merged_ref, factor_ref, weight_1, error, sem
):
    rank = seed_ref.shape[1]
    step = width // TILES
    tiles = [slice(i * step, (i + 1) * step) for i in range(TILES)]
    fetch = pltpu.make_async_copy(weight_hbm, weight_1, sem.at[TILES])
    fetch.start()
    loads = [
        pltpu.make_async_copy(error_hbm.at[rows], error.at[rows], sem.at[i]) for i, rows in enumerate(tiles)
    ]
    for load in loads:
        load.start()
    x = arrived_ref[:, :width]
    half = weight_1.shape[1]

    def columns(weight, lanes):
        pre = nn(x, weight[...])
        s = 1.0 / (1.0 + jnp.exp(-pre))
        grad = arrived_ref[:, width + lanes.start : width + lanes.stop].astype(f32)
        grad_pre_ref[:, lanes] = (grad * (s * (1.0 + pre * (1.0 - s)))).astype(bf16)

    columns(weight_0, slice(0, half))
    fetch.wait()
    columns(weight_1, slice(half, 2 * half))
    grad_pre = grad_pre_ref[...]
    high, low = halves(seed_ref[...])
    both = jnp.concatenate([high, low], axis=1)
    for i, rows in enumerate(tiles):
        loads[i].wait()
        upper, lower = halves(tn(arrived_ref[:, rows], grad_pre) + error[rows, :].astype(f32))
        merged_ref[rows, :] = upper
        part = nn(upper, both)
        part = part[:, :rank] + part[:, rank:] + nn(lower, high)
        part = part.T
        for j in range(step // LANES):
            factor_ref[:, i * (step // LANES) + j, :] = part[:, j * LANES : (j + 1) * LANES]


def rows_kernel(grad_pre_ref, weight_0, weight_1, grad_rows_ref):
    half = weight_0.shape[1]
    rows = nt(grad_pre_ref[:, :half], weight_0[...]) + nt(grad_pre_ref[:, half:], weight_1[...])
    grad_rows_ref[...] = rows.astype(bf16)


def sum_and_copy_kernel(parts_ref, copies_ref):
    total = jnp.sum(parts_ref[...], axis=0)
    copies_ref[...] = jnp.broadcast_to(total[None], copies_ref.shape)


def right_kernel(factor_ref, merged_ref, right_ref):
    rank, blocks, _ = factor_ref.shape
    step = 2 * LANES
    total = jnp.zeros(right_ref.shape, f32)
    for i in range(blocks // 2):
        pair = jnp.concatenate([factor_ref[:, 2 * i, :], factor_ref[:, 2 * i + 1, :]], axis=1)
        both = jnp.concatenate(halves(pair), axis=0)
        part = nn(both, merged_ref[i * step : (i + 1) * step, :])
        total = total + part[:rank] + part[rank:]
    right_ref[...] = total


def left_kernel(factor_ref, left_ref, gathered_ref):
    rank, blocks, _ = factor_ref.shape
    for j in range(blocks):
        gathered_ref[:, j * LANES : (j + 1) * LANES] = factor_ref[:, j, :]
    high, low = halves(gathered_ref[...])
    gram = nt(high, high) + nt(high, low) + nt(low, high)
    line = lax.broadcasted_iota(jnp.int32, (rank, rank), 0)
    column = lax.broadcasted_iota(jnp.int32, (rank, rank), 1)
    both = jnp.concatenate([gram, (line == column).astype(f32)], axis=1)
    own = lax.broadcasted_iota(jnp.int32, both.shape, 0)
    for i in range(rank):
        row = both[i : i + 1, :] / both[i : i + 1, i : i + 1]
        both = jnp.where(own == i, row, both - both[:, i : i + 1] * row)
    upper, lower = halves(both[:, rank:])
    left_ref[...] = nn(upper, high) + nn(upper, low) + nn(lower, high)


def finish_kernel(
    count, total_ref, left_ref, mine_ref, merged_hbm, error_hbm, weight_ref, merged, error, load_sem, store_sem
):
    step = merged.shape[0] // TILES
    tiles = [slice(i * step, (i + 1) * step) for i in range(TILES)]
    loads = [
        pltpu.make_async_copy(merged_hbm.at[rows], merged.at[rows], load_sem.at[i])
        for i, rows in enumerate(tiles)
    ]
    for load in loads:
        load.start()
    high, low = halves(total_ref[...] / count)
    right = jnp.concatenate([high, low, high], axis=0)
    upper, lower = halves(mine_ref[...])
    weight_ref[...] = tn(jnp.concatenate([upper, upper, lower], axis=0), right)
    stores = []
    for i, rows in enumerate(tiles):
        upper, lower = halves(left_ref[:, rows])
        low_rank = tn(jnp.concatenate([upper, upper, lower], axis=0), right)
        loads[i].wait()
        error[rows, :] = (merged[rows, :].astype(f32) - low_rank).astype(bf16)
        stores.append(pltpu.make_async_copy(error.at[rows], error_hbm.at[rows], store_sem.at[i]))
        stores[i].start()
    for store in stores:
        store.wait()


def combine_kernel(select_ref, gates_ref, returned_ref, out_hbm, out, store_sem):
    rows, width = out.shape
    step = width // TILES
    tiles = [slice(i * step, (i + 1) * step) for i in range(TILES)]
    gates = gates_ref[...]
    stores = []
    for i, c in enumerate(tiles):
        picked = nn(select_ref[...], returned_ref[:, c])
        out[:, c] = (picked[:rows] * gates[:, 0:1] + picked[rows:] * gates[:, 1:2]).astype(bf16)
        stores.append(pltpu.make_async_copy(out.at[:, c], out_hbm.at[:, c], store_sem.at[i]))
        stores[i].start()
    for store in stores:
        store.wait()


def shape(dims, dtype):
    return jax.ShapeDtypeStruct(dims, dtype)


def partners(size):
    steps = [1 << k for k in range(size.bit_length() - 1)]
    if len(steps) > 1:
        steps[-1] = size - 1
    return steps


def from_partner(x, axis, step):
    return lax.ppermute(x, axis, [(i, i ^ step) for i in range(lax.axis_size(axis))])


def body(tokens, routes, gates, grad_hidden, w_in, error, q_seed):
    experts = lax.axis_size("expert")
    replicas = lax.axis_size(DP)
    row_count, width = tokens.shape
    hidden = grad_hidden.shape[2]
    rank = q_seed.shape[2]
    capacity = 4 * row_count // experts
    slots = experts * capacity
    routes_t = routes.T
    dma = pltpu.SemaphoreType.DMA

    sent = call(
        lambda *refs: prepare_kernel(experts, capacity, *refs),
        shape((slots, width + hidden), bf16),
        (routes_t, gates.T, tokens, grad_hidden.reshape(row_count, 2 * hidden)),
        room=FULL,
        in_specs=[HBM, HBM, HBM, HBM],
        out_specs=HBM,
        scratch_shapes=[
            pltpu.VMEM((2, row_count), jnp.int32),
            pltpu.VMEM((2, row_count), f32),
            pltpu.VMEM((row_count, width), bf16),
            pltpu.VMEM((row_count, 2 * hidden), bf16),
            pltpu.VMEM((slots, width + hidden), bf16),
            dma((8,)),
        ],
    )
    w_mine, sent = lax.optimization_barrier((w_in[0], sent))
    arrived = lax.all_to_all(
        sent.reshape(experts, capacity, width + hidden), "expert", 0, 0, tiled=True
    ).reshape(slots, width + hidden)
    weight = lax.all_gather(w_mine, DP[1], tiled=True)
    select = call(
        lambda *refs: select_kernel(experts, capacity, *refs),
        shape((2 * row_count, slots), bf16),
        (routes_t,),
    )
    weight, select = lax.optimization_barrier((weight, select))
    half = hidden // 2
    weight_0 = lax.all_gather(weight[:, :half], DP[0], tiled=True)
    weight_1 = lax.all_gather(weight[:, half:], DP[0], tiled=True)

    blocks = width // LANES
    grad_pre, merged, factor = call(
        lambda *refs: merge_kernel(width, *refs),
        (
            shape((slots, hidden), bf16),
            shape((width, hidden), bf16),
            shape((rank, blocks, LANES), f32),
        ),
        (arrived, weight_0, weight_1, error[0, 0], q_seed[0]),
        room=ROOM,
        in_specs=[VMEM, VMEM, HBM, HBM, VMEM],
        out_specs=[VMEM, VMEM, VMEM],
        scratch_shapes=[pltpu.VMEM((width, half), bf16), pltpu.VMEM((width, hidden), bf16), dma((TILES + 1,))],
    )
    each = rank // replicas
    parts = lax.all_to_all(factor, DP, 0, 0, tiled=True)
    grad_rows = call(rows_kernel, shape((slots, width), bf16), (grad_pre, weight_0, weight_1))
    copies = call(
        sum_and_copy_kernel,
        shape((replicas, each * blocks, LANES), f32),
        (parts.reshape(replicas, each * blocks, LANES),),
    )
    factor = lax.all_to_all(copies, DP, 0, 0, tiled=True).reshape(rank, blocks, LANES)
    right = call(right_kernel, shape((rank, hidden), f32), (factor, merged))
    right, grad_rows = lax.optimization_barrier((right, grad_rows))
    returned = lax.all_to_all(
        grad_rows.reshape(experts, capacity, width), "expert", 0, 0, tiled=True
    ).reshape(slots, width)

    left = call(
        left_kernel,
        shape((rank, width), f32),
        (factor,),
        scratch_shapes=[pltpu.VMEM((rank, width), f32)],
    )
    shard = width // replicas
    mine = lax.dynamic_slice_in_dim(left, lax.axis_index(DP) * shard, shard, 1)
    steps = [(axis, step) for axis in DP[::-1] for step in partners(lax.axis_size(axis))]
    for i, (axis, step) in enumerate(steps):
        other = from_partner(right, axis, step)
        if i == len(steps) - 3:
            other, left = lax.optimization_barrier((other, left))
        if i == len(steps) - 2:
            other, mine = lax.optimization_barrier((other, mine))
        right = right + other
    error_next, weight_grad = call(
        lambda *refs: finish_kernel(replicas, *refs),
        (shape((width, hidden), bf16), shape((shard, hidden), f32)),
        (right, left, mine, merged),
        room=FULL,
        in_specs=[VMEM, VMEM, VMEM, HBM],
        out_specs=[HBM, VMEM],
        scratch_shapes=[
            pltpu.VMEM((width, hidden), bf16),
            pltpu.VMEM((width, hidden), bf16),
            dma((TILES,)),
            dma((TILES,)),
        ],
    )
    grad_tokens = call(
        combine_kernel,
        shape((row_count, width), bf16),
        (select, gates, returned),
        in_specs=[VMEM, VMEM, VMEM],
        out_specs=HBM,
        scratch_shapes=[pltpu.VMEM((row_count, width), bf16), dma((TILES,))],
    )
    return grad_tokens, error_next[None, None], weight_grad[None]


def solution(mesh):
    torus = Mesh(mesh.devices.reshape(4, 8, mesh.shape["expert"]), DP_EXPERT)
    in_specs = (
        P(DP_EXPERT, None),
        P(DP_EXPERT, None),
        P(DP_EXPERT, None),
        P(DP_EXPERT, None, None),
        P("expert", DP, None),
        P(DP, "expert", None, None),
        P("expert", None, None),
    )
    out_specs = (P(DP_EXPERT, None), P(DP, "expert", None, None), P("expert", DP, None))
    return jax.shard_map(body, mesh=torus, in_specs=in_specs, out_specs=out_specs, check_vma=False)
```

```python
import jax
import jax.numpy as jnp
from jax import lax
from jax.experimental import pallas as pl
from jax.experimental.pallas import tpu as pltpu
from jax.sharding import Mesh
from jax.sharding import PartitionSpec as P

DP = ("dp_0", "dp_1")
DP_EXPERT = ("dp_0", "dp_1", "expert")

f32, bf16 = jnp.float32, jnp.bfloat16
HBM = pl.BlockSpec(memory_space=pltpu.HBM)
VMEM = pl.BlockSpec(memory_space=pltpu.VMEM)
TILES = 7
ROOM = 16_000_000
FULL = 63_400_000
LANES = 128


def nn(a, b):
    return lax.dot_general(a, b, (((1,), (0,)), ((), ())), preferred_element_type=f32)


def nt(a, b):
    return lax.dot_general(a, b, (((1,), (1,)), ((), ())), preferred_element_type=f32)


def tn(a, b):
    return lax.dot_general(a, b, (((0,), (0,)), ((), ())), preferred_element_type=f32)


def halves(x):
    high = x.astype(bf16)
    return high, (x - high.astype(f32)).astype(bf16)


def call(kernel, outs, args, room=ROOM, **more):
    return pl.pallas_call(
        kernel,
        out_shape=outs,
        compiler_params=pltpu.CompilerParams(vmem_limit_bytes=room),
        cost_estimate=pl.CostEstimate(flops=0, bytes_accessed=0, transcendentals=0),
        **more,
    )(*args)


def one_hots(routes, experts, capacity):
    rows = routes.shape[1]
    slots = experts * capacity
    before = (
        lax.broadcasted_iota(jnp.int32, (rows, rows), 0) < lax.broadcasted_iota(jnp.int32, (rows, rows), 1)
    ).astype(bf16)
    expert = lax.broadcasted_iota(jnp.int32, (experts, rows), 0)
    slot = lax.broadcasted_iota(jnp.int32, (slots, rows), 0)
    started = jnp.zeros((experts, 1), f32)
    out = []
    for k in range(2):
        chosen = routes[k : k + 1, :]
        match = (expert == chosen).astype(f32)
        earlier = nn(match.astype(bf16), before) + started
        place = jnp.sum(match * earlier, axis=0, keepdims=True).astype(jnp.int32) + chosen * capacity
        out.append((slot == place).astype(f32))
        started = started + jnp.sum(match, axis=1, keepdims=True)
    return out


def prepare_kernel(
    experts, capacity, routes_hbm, gates_hbm, tokens_hbm, grad_hbm, sent_hbm, routes, gates, tokens, grad, sent, sem
):
    width = tokens.shape[1]
    hidden = grad.shape[1] // 2
    copies = [
        pltpu.make_async_copy(routes_hbm, routes, sem.at[0]),
        pltpu.make_async_copy(gates_hbm, gates, sem.at[1]),
        pltpu.make_async_copy(tokens_hbm, tokens, sem.at[2]),
        pltpu.make_async_copy(grad_hbm, grad, sem.at[3]),
    ]
    for copy in copies:
        copy.start()
    copies[0].wait()
    first, second = one_hots(routes[...], experts, capacity)
    copies[1].wait()
    gate = jnp.sum(first * gates[0:1, :] + second * gates[1:2, :], axis=1, keepdims=True)
    either, first, second = (first + second).astype(bf16), first.astype(bf16), second.astype(bf16)
    copies[2].wait()
    copies[3].wait()
    parts = 4
    step = first.shape[0] // parts
    done = []
    for i in range(parts):
        rows = slice(i * step, (i + 1) * step)
        sent[rows, :width] = (nn(either[rows], tokens[...]) * gate[rows]).astype(bf16)
        grads = nn(first[rows], grad[:, :hidden]) + nn(second[rows], grad[:, hidden:])
        sent[rows, width:] = grads.astype(bf16)
        copy = pltpu.make_async_copy(sent.at[rows], sent_hbm.at[rows], sem.at[4 + i])
        copy.start()
        done.append(copy)
    for copy in done:
        copy.wait()


def select_kernel(experts, capacity, routes_ref, select_ref):
    rows = routes_ref.shape[1]
    for k, places in enumerate(one_hots(routes_ref[...], experts, capacity)):
        select_ref[k * rows : (k + 1) * rows, :] = places.T.astype(bf16)


def merge_kernel(
    width, arrived_ref, weight_0, weight_1, error_ref, seed_ref, grad_pre_ref, merged_ref, factor_ref
):
    rank = seed_ref.shape[1]
    step = width // TILES
    tiles = [slice(i * step, (i + 1) * step) for i in range(TILES)]
    x = arrived_ref[:, :width]
    half = weight_1.shape[1]

    def columns(weight, lanes):
        pre = nn(x, weight[...])
        s = 1.0 / (1.0 + jnp.exp(-pre))
        grad = arrived_ref[:, width + lanes.start : width + lanes.stop].astype(f32)
        grad_pre_ref[:, lanes] = (grad * (s * (1.0 + pre * (1.0 - s)))).astype(bf16)

    columns(weight_0, slice(0, half))
    columns(weight_1, slice(half, 2 * half))
    grad_pre = grad_pre_ref[...]
    high, low = halves(seed_ref[...])
    both = jnp.concatenate([high, low], axis=1)
    for i, rows in enumerate(tiles):
        upper, lower = halves(tn(arrived_ref[:, rows], grad_pre) + error_ref[rows, :].astype(f32))
        merged_ref[rows, :] = upper
        part = nn(upper, both)
        part = part[:, :rank] + part[:, rank:] + nn(lower, high)
        part = part.T
        for j in range(step // LANES):
            factor_ref[:, i * (step // LANES) + j, :] = part[:, j * LANES : (j + 1) * LANES]


def rows_kernel(grad_pre_ref, weight_0, weight_1, grad_rows_ref):
    half = weight_0.shape[1]
    rows = nt(grad_pre_ref[:, :half], weight_0[...]) + nt(grad_pre_ref[:, half:], weight_1[...])
    grad_rows_ref[...] = rows.astype(bf16)


def sum_and_copy_kernel(parts_ref, copies_ref):
    total = jnp.sum(parts_ref[...], axis=0)
    copies_ref[...] = jnp.broadcast_to(total[None], copies_ref.shape)


def right_kernel(factor_ref, merged_ref, right_ref):
    rank, blocks, _ = factor_ref.shape
    step = 2 * LANES
    total = jnp.zeros(right_ref.shape, f32)
    for i in range(blocks // 2):
        pair = jnp.concatenate([factor_ref[:, 2 * i, :], factor_ref[:, 2 * i + 1, :]], axis=1)
        both = jnp.concatenate(halves(pair), axis=0)
        part = nn(both, merged_ref[i * step : (i + 1) * step, :])
        total = total + part[:rank] + part[rank:]
    right_ref[...] = total


def left_kernel(factor_ref, left_ref, gathered_ref):
    rank, blocks, _ = factor_ref.shape
    for j in range(blocks):
        gathered_ref[:, j * LANES : (j + 1) * LANES] = factor_ref[:, j, :]
    high, low = halves(gathered_ref[...])
    gram = nt(high, high) + nt(high, low) + nt(low, high)
    line = lax.broadcasted_iota(jnp.int32, (rank, rank), 0)
    column = lax.broadcasted_iota(jnp.int32, (rank, rank), 1)
    both = jnp.concatenate([gram, (line == column).astype(f32)], axis=1)
    own = lax.broadcasted_iota(jnp.int32, both.shape, 0)
    for i in range(rank):
        row = both[i : i + 1, :] / both[i : i + 1, i : i + 1]
        both = jnp.where(own == i, row, both - both[:, i : i + 1] * row)
    upper, lower = halves(both[:, rank:])
    left = (nn(upper, high) + nn(upper, low) + nn(lower, high)).T
    upper, lower = halves(left)
    left_ref[...] = jnp.concatenate([upper, upper, lower], axis=1)


def finish_kernel(
    count, total_ref, left_ref, mine_ref, merged_hbm, error_hbm, weight_ref, merged, error, load_sem, store_sem
):
    step = merged.shape[0] // TILES
    tiles = [slice(i * step, (i + 1) * step) for i in range(TILES)]
    loads = [
        pltpu.make_async_copy(merged_hbm.at[rows], merged.at[rows], load_sem.at[i])
        for i, rows in enumerate(tiles)
    ]
    for load in loads:
        load.start()
    high, low = halves(total_ref[...] / count)
    right = jnp.concatenate([high, low, high], axis=0)
    weight_ref[...] = nn(mine_ref[...], right)
    stores = []
    for i, rows in enumerate(tiles):
        low_rank = nn(left_ref[rows, :], right)
        loads[i].wait()
        error[rows, :] = (merged[rows, :].astype(f32) - low_rank).astype(bf16)
        stores.append(pltpu.make_async_copy(error.at[rows], error_hbm.at[rows], store_sem.at[i]))
        stores[i].start()
    for store in stores:
        store.wait()


def combine_kernel(select_ref, gates_ref, returned_ref, out_hbm, out, store_sem):
    rows, width = out.shape
    step = width // TILES
    tiles = [slice(i * step, (i + 1) * step) for i in range(TILES)]
    gates = gates_ref[...]
    stores = []
    for i, c in enumerate(tiles):
        picked = nn(select_ref[...], returned_ref[:, c])
        out[:, c] = (picked[:rows] * gates[:, 0:1] + picked[rows:] * gates[:, 1:2]).astype(bf16)
        stores.append(pltpu.make_async_copy(out.at[:, c], out_hbm.at[:, c], store_sem.at[i]))
        stores[i].start()
    for store in stores:
        store.wait()


def shape(dims, dtype):
    return jax.ShapeDtypeStruct(dims, dtype)


def partners(size):
    steps = [1 << k for k in range(size.bit_length() - 1)]
    if len(steps) > 1:
        steps[-1] = size - 1
    return steps


def from_partner(x, axis, step):
    return lax.ppermute(x, axis, [(i, i ^ step) for i in range(lax.axis_size(axis))])


def body(tokens, routes, gates, grad_hidden, w_in, error, q_seed):
    experts = lax.axis_size("expert")
    replicas = lax.axis_size(DP)
    row_count, width = tokens.shape
    hidden = grad_hidden.shape[2]
    rank = q_seed.shape[2]
    capacity = 4 * row_count // experts
    slots = experts * capacity
    routes_t = routes.T
    dma = pltpu.SemaphoreType.DMA

    sent = call(
        lambda *refs: prepare_kernel(experts, capacity, *refs),
        shape((slots, width + hidden), bf16),
        (routes_t, gates.T, tokens, grad_hidden.reshape(row_count, 2 * hidden)),
        room=FULL,
        in_specs=[HBM, HBM, HBM, HBM],
        out_specs=HBM,
        scratch_shapes=[
            pltpu.VMEM((2, row_count), jnp.int32),
            pltpu.VMEM((2, row_count), f32),
            pltpu.VMEM((row_count, width), bf16),
            pltpu.VMEM((row_count, 2 * hidden), bf16),
            pltpu.VMEM((slots, width + hidden), bf16),
            dma((8,)),
        ],
    )
    w_mine, sent = lax.optimization_barrier((w_in[0], sent))
    arrived = lax.all_to_all(
        sent.reshape(experts, capacity, width + hidden), "expert", 0, 0, tiled=True
    ).reshape(slots, width + hidden)
    weight = lax.all_gather(w_mine, DP[1], tiled=True)
    half = hidden // 2
    weight_0 = lax.all_gather(weight[:, :half], DP[0], tiled=True)
    weight_1 = lax.all_gather(weight[:, half:], DP[0], tiled=True)

    blocks = width // LANES
    grad_pre, merged, factor = call(
        lambda *refs: merge_kernel(width, *refs),
        (
            shape((slots, hidden), bf16),
            shape((width, hidden), bf16),
            shape((rank, blocks, LANES), f32),
        ),
        (arrived, weight_0, weight_1, error[0, 0], q_seed[0]),
    )
    each = rank // replicas
    parts = lax.all_to_all(factor, DP, 0, 0, tiled=True)
    grad_rows = call(rows_kernel, shape((slots, width), bf16), (grad_pre, weight_0, weight_1))
    copies = call(
        sum_and_copy_kernel,
        shape((replicas, each * blocks, LANES), f32),
        (parts.reshape(replicas, each * blocks, LANES),),
    )
    factor = lax.all_to_all(copies, DP, 0, 0, tiled=True).reshape(rank, blocks, LANES)
    factor, grad_rows = lax.optimization_barrier((factor, grad_rows))
    returned = lax.all_to_all(
        grad_rows.reshape(experts, capacity, width), "expert", 0, 0, tiled=True
    ).reshape(slots, width)

    right = call(right_kernel, shape((rank, hidden), f32), (factor, merged))
    left = call(
        left_kernel,
        shape((width, 3 * rank), bf16),
        (factor,),
        scratch_shapes=[pltpu.VMEM((rank, width), f32)],
    )
    shard = width // replicas
    mine = lax.dynamic_slice_in_dim(left, lax.axis_index(DP) * shard, shard, 0)
    select = call(
        lambda *refs: select_kernel(experts, capacity, *refs),
        shape((2 * row_count, slots), bf16),
        (routes_t,),
    )
    steps = [(axis, step) for axis in DP[::-1] for step in partners(lax.axis_size(axis))]
    for i, (axis, step) in enumerate(steps):
        other = from_partner(right, axis, step)
        if i == len(steps) - 4:
            other, select = lax.optimization_barrier((other, select))
        if i == len(steps) - 3:
            other, left = lax.optimization_barrier((other, left))
        if i == len(steps) - 2:
            other, mine = lax.optimization_barrier((other, mine))
        right = right + other
    error_next, weight_grad = call(
        lambda *refs: finish_kernel(replicas, *refs),
        (shape((width, hidden), bf16), shape((shard, hidden), f32)),
        (right, left, mine, merged),
        room=FULL,
        in_specs=[VMEM, VMEM, VMEM, HBM],
        out_specs=[HBM, VMEM],
        scratch_shapes=[
            pltpu.VMEM((width, hidden), bf16),
            pltpu.VMEM((width, hidden), bf16),
            dma((TILES,)),
            dma((TILES,)),
        ],
    )
    grad_tokens = call(
        combine_kernel,
        shape((row_count, width), bf16),
        (select, gates, returned),
        in_specs=[VMEM, VMEM, VMEM],
        out_specs=HBM,
        scratch_shapes=[pltpu.VMEM((row_count, width), bf16), dma((TILES,))],
    )
    return grad_tokens, error_next[None, None], weight_grad[None]


def solution(mesh):
    torus = Mesh(mesh.devices.reshape(4, 8, mesh.shape["expert"]), DP_EXPERT)
    in_specs = (
        P(DP_EXPERT, None),
        P(DP_EXPERT, None),
        P(DP_EXPERT, None),
        P(DP_EXPERT, None, None),
        P("expert", DP, None),
        P(DP, "expert", None, None),
        P("expert", None, None),
    )
    out_specs = (P(DP_EXPERT, None), P(DP, "expert", None, None), P("expert", DP, None))
    return jax.shard_map(body, mesh=torus, in_specs=in_specs, out_specs=out_specs, check_vma=False)
```

```python
import jax
import jax.numpy as jnp
from jax import lax
from jax.experimental import pallas as pl
from jax.experimental.pallas import tpu as pltpu
from jax.sharding import Mesh
from jax.sharding import PartitionSpec as P

DP = ("dp_0", "dp_1")
DP_EXPERT = ("dp_0", "dp_1", "expert")

f32, bf16 = jnp.float32, jnp.bfloat16
HBM = pl.BlockSpec(memory_space=pltpu.HBM)
VMEM = pl.BlockSpec(memory_space=pltpu.VMEM)
TILES = 7
ROOM = 16_000_000
FULL = 63_400_000
LANES = 128


def nn(a, b):
    return lax.dot_general(a, b, (((1,), (0,)), ((), ())), preferred_element_type=f32)


def nt(a, b):
    return lax.dot_general(a, b, (((1,), (1,)), ((), ())), preferred_element_type=f32)


def tn(a, b):
    return lax.dot_general(a, b, (((0,), (0,)), ((), ())), preferred_element_type=f32)


def halves(x):
    high = x.astype(bf16)
    return high, (x - high.astype(f32)).astype(bf16)


def call(kernel, outs, args, room=ROOM, **more):
    return pl.pallas_call(
        kernel,
        out_shape=outs,
        compiler_params=pltpu.CompilerParams(vmem_limit_bytes=room),
        cost_estimate=pl.CostEstimate(flops=0, bytes_accessed=0, transcendentals=0),
        **more,
    )(*args)


def one_hots(routes, experts, capacity):
    rows = routes.shape[1]
    slots = experts * capacity
    before = (
        lax.broadcasted_iota(jnp.int32, (rows, rows), 0) < lax.broadcasted_iota(jnp.int32, (rows, rows), 1)
    ).astype(bf16)
    expert = lax.broadcasted_iota(jnp.int32, (experts, rows), 0)
    slot = lax.broadcasted_iota(jnp.int32, (slots, rows), 0)
    started = jnp.zeros((experts, 1), f32)
    out = []
    for k in range(2):
        chosen = routes[k : k + 1, :]
        match = (expert == chosen).astype(f32)
        earlier = nn(match.astype(bf16), before) + started
        place = jnp.sum(match * earlier, axis=0, keepdims=True).astype(jnp.int32) + chosen * capacity
        out.append((slot == place).astype(f32))
        started = started + jnp.sum(match, axis=1, keepdims=True)
    return out


def prepare_kernel(
    experts, capacity, routes_hbm, gates_hbm, tokens_hbm, grad_hbm, sent_hbm, routes, gates, tokens, grad, sent, sem
):
    width = tokens.shape[1]
    hidden = grad.shape[2]
    copies = [
        pltpu.make_async_copy(routes_hbm, routes, sem.at[0]),
        pltpu.make_async_copy(gates_hbm, gates, sem.at[1]),
        pltpu.make_async_copy(tokens_hbm, tokens, sem.at[2]),
        pltpu.make_async_copy(grad_hbm, grad, sem.at[3]),
    ]
    for copy in copies:
        copy.start()
    copies[0].wait()
    first, second = one_hots(routes[...], experts, capacity)
    copies[1].wait()
    gate = jnp.sum(first * gates[0:1, :] + second * gates[1:2, :], axis=1, keepdims=True)
    either, first, second = (first + second).astype(bf16), first.astype(bf16), second.astype(bf16)
    copies[3].wait()
    pairs = grad[...]
    grad_0, grad_1 = pairs[:, 0, :], pairs[:, 1, :]
    copies[2].wait()
    parts = 4
    step = first.shape[0] // parts
    done = []
    for i in range(parts):
        rows = slice(i * step, (i + 1) * step)
        sent[rows, :width] = (nn(either[rows], tokens[...]) * gate[rows]).astype(bf16)
        grads = nn(first[rows], grad_0) + nn(second[rows], grad_1)
        sent[rows, width:] = grads.astype(bf16)
        copy = pltpu.make_async_copy(sent.at[rows], sent_hbm.at[rows], sem.at[4 + i])
        copy.start()
        done.append(copy)
    for copy in done:
        copy.wait()


def select_kernel(experts, capacity, routes_ref, select_ref):
    rows = routes_ref.shape[1]
    for k, places in enumerate(one_hots(routes_ref[...], experts, capacity)):
        select_ref[k * rows : (k + 1) * rows, :] = places.T.astype(bf16)


def seeded_kernel(error_ref, seed_ref, seeded_ref):
    rank = seed_ref.shape[1]
    part = nn(error_ref[...], jnp.concatenate(halves(seed_ref[...]), axis=1))
    seeded_ref[...] = (part[:, :rank] + part[:, rank:]).T


def factor_kernel(width, arrived_ref, weight_0, weight_1, seed_ref, seeded_ref, grad_pre_ref, factor_ref):
    rank = seed_ref.shape[1]
    x = arrived_ref[:, :width]
    start = 0
    for weight in (weight_0, weight_1):
        lanes = slice(start, start + weight.shape[1])
        pre = nn(x, weight[...])
        s = 1.0 / (1.0 + jnp.exp(-pre))
        grad = arrived_ref[:, width + lanes.start : width + lanes.stop].astype(f32)
        grad_pre_ref[:, lanes] = (grad * (s * (1.0 + pre * (1.0 - s)))).astype(bf16)
        start = lanes.stop
    row = nn(grad_pre_ref[...], jnp.concatenate(halves(seed_ref[...]), axis=1))
    part = tn(jnp.concatenate(halves(row[:, :rank] + row[:, rank:]), axis=1), x)
    factor = part[:rank] + part[rank:] + seeded_ref[...]
    for j in range(width // LANES):
        factor_ref[:, j, :] = factor[:, j * LANES : (j + 1) * LANES]


def merge_kernel(width, arrived_ref, grad_pre_ref, error_ref, merged_ref):
    step = width // TILES
    grad_pre = grad_pre_ref[...]
    for i in range(TILES):
        rows = slice(i * step, (i + 1) * step)
        merged = tn(arrived_ref[:, rows], grad_pre) + error_ref[rows, :].astype(f32)
        merged_ref[rows, :] = merged.astype(bf16)


def rows_kernel(grad_pre_ref, weight_0, weight_1, grad_rows_ref):
    half = weight_0.shape[1]
    rows = nt(grad_pre_ref[:, :half], weight_0[...]) + nt(grad_pre_ref[:, half:], weight_1[...])
    grad_rows_ref[...] = rows.astype(bf16)


def sum_and_copy_kernel(parts_ref, copies_ref):
    total = jnp.sum(parts_ref[...], axis=0)
    copies_ref[...] = jnp.broadcast_to(total[None], copies_ref.shape)


def right_kernel(factor_ref, merged_ref, right_ref):
    rank, blocks, _ = factor_ref.shape
    step = 2 * LANES
    total = jnp.zeros(right_ref.shape, f32)
    for i in range(blocks // 2):
        pair = jnp.concatenate([factor_ref[:, 2 * i, :], factor_ref[:, 2 * i + 1, :]], axis=1)
        both = jnp.concatenate(halves(pair), axis=0)
        part = nn(both, merged_ref[i * step : (i + 1) * step, :])
        total = total + part[:rank] + part[rank:]
    right_ref[...] = total


def left_kernel(factor_ref, left_ref, gathered_ref):
    rank, blocks, _ = factor_ref.shape
    for j in range(blocks):
        gathered_ref[:, j * LANES : (j + 1) * LANES] = factor_ref[:, j, :]
    high, low = halves(gathered_ref[...])
    gram = nt(high, high) + nt(high, low) + nt(low, high)
    line = lax.broadcasted_iota(jnp.int32, (rank, rank), 0)
    column = lax.broadcasted_iota(jnp.int32, (rank, rank), 1)
    both = jnp.concatenate([gram, (line == column).astype(f32)], axis=1)
    own = lax.broadcasted_iota(jnp.int32, both.shape, 0)
    for i in range(rank):
        row = both[i : i + 1, :] / both[i : i + 1, i : i + 1]
        both = jnp.where(own == i, row, both - both[:, i : i + 1] * row)
    upper, lower = halves(both[:, rank:])
    left = (nn(upper, high) + nn(upper, low) + nn(lower, high)).T
    upper, lower = halves(left)
    left_ref[...] = jnp.concatenate([upper, upper, lower], axis=1)


def finish_kernel(
    count, total_ref, left_ref, mine_ref, merged_hbm, error_hbm, weight_ref, merged, error, load_sem, store_sem
):
    step = merged.shape[0] // TILES
    tiles = [slice(i * step, (i + 1) * step) for i in range(TILES)]
    loads = [
        pltpu.make_async_copy(merged_hbm.at[rows], merged.at[rows], load_sem.at[i])
        for i, rows in enumerate(tiles)
    ]
    for load in loads:
        load.start()
    high, low = halves(total_ref[...] / count)
    right = jnp.concatenate([high, low, high], axis=0)
    weight_ref[...] = nn(mine_ref[...], right)
    stores = []
    for i, rows in enumerate(tiles):
        low_rank = nn(left_ref[rows, :], right)
        loads[i].wait()
        error[rows, :] = (merged[rows, :].astype(f32) - low_rank).astype(bf16)
        stores.append(pltpu.make_async_copy(error.at[rows], error_hbm.at[rows], store_sem.at[i]))
        stores[i].start()
    for store in stores:
        store.wait()


def combine_kernel(select_ref, gates_ref, returned_ref, out_hbm, out, store_sem):
    rows, width = out.shape
    step = width // TILES
    tiles = [slice(i * step, (i + 1) * step) for i in range(TILES)]
    gates = gates_ref[...]
    stores = []
    for i, c in enumerate(tiles):
        picked = nn(select_ref[...], returned_ref[:, c])
        out[:, c] = (picked[:rows] * gates[:, 0:1] + picked[rows:] * gates[:, 1:2]).astype(bf16)
        stores.append(pltpu.make_async_copy(out.at[:, c], out_hbm.at[:, c], store_sem.at[i]))
        stores[i].start()
    for store in stores:
        store.wait()


def shape(dims, dtype):
    return jax.ShapeDtypeStruct(dims, dtype)


def partners(size):
    steps = [1 << k for k in range(size.bit_length() - 1)]
    if len(steps) > 1:
        steps[-1] = size - 1
    return steps


def from_partner(x, axis, step):
    return lax.ppermute(x, axis, [(i, i ^ step) for i in range(lax.axis_size(axis))])


def body(tokens, routes, gates, grad_hidden, w_in, error, q_seed):
    experts = lax.axis_size("expert")
    replicas = lax.axis_size(DP)
    row_count, width = tokens.shape
    hidden = grad_hidden.shape[2]
    rank = q_seed.shape[2]
    capacity = 4 * row_count // experts
    slots = experts * capacity
    routes_t = routes.T
    dma = pltpu.SemaphoreType.DMA

    sent = call(
        lambda *refs: prepare_kernel(experts, capacity, *refs),
        shape((slots, width + hidden), bf16),
        (routes_t, gates.T, tokens, grad_hidden),
        room=FULL,
        in_specs=[HBM, HBM, HBM, HBM],
        out_specs=HBM,
        scratch_shapes=[
            pltpu.VMEM((2, row_count), jnp.int32),
            pltpu.VMEM((2, row_count), f32),
            pltpu.VMEM((row_count, width), bf16),
            pltpu.VMEM((row_count, 2, hidden), bf16),
            pltpu.VMEM((slots, width + hidden), bf16),
            dma((8,)),
        ],
    )
    w_mine, sent = lax.optimization_barrier((w_in[0], sent))
    arrived = lax.all_to_all(
        sent.reshape(experts, capacity, width + hidden), "expert", 0, 0, tiled=True
    ).reshape(slots, width + hidden)
    weight = lax.all_gather(w_mine, DP[1], tiled=True)
    seeded = call(seeded_kernel, shape((rank, width), f32), (error[0, 0], q_seed[0]))
    most = 3 * hidden // 4
    rest, seeded = lax.optimization_barrier((weight[:, most:], seeded))
    weight_0 = lax.all_gather(weight[:, :most], DP[0], tiled=True)
    weight_1 = lax.all_gather(rest, DP[0], tiled=True)

    blocks = width // LANES
    grad_pre, factor = call(
        lambda *refs: factor_kernel(width, *refs),
        (shape((slots, hidden), bf16), shape((rank, blocks, LANES), f32)),
        (arrived, weight_0, weight_1, q_seed[0], seeded),
    )
    each = rank // replicas
    parts = lax.all_to_all(factor, DP, 0, 0, tiled=True)
    merged = call(
        lambda *refs: merge_kernel(width, *refs), shape((width, hidden), bf16), (arrived, grad_pre, error[0, 0])
    )
    grad_rows = call(rows_kernel, shape((slots, width), bf16), (grad_pre, weight_0, weight_1))
    copies = call(
        sum_and_copy_kernel,
        shape((replicas, each * blocks, LANES), f32),
        (parts.reshape(replicas, each * blocks, LANES),),
    )
    factor = lax.all_to_all(copies, DP, 0, 0, tiled=True).reshape(rank, blocks, LANES)
    factor, grad_rows, merged = lax.optimization_barrier((factor, grad_rows, merged))
    returned = lax.all_to_all(
        grad_rows.reshape(experts, capacity, width), "expert", 0, 0, tiled=True
    ).reshape(slots, width)

    right = call(right_kernel, shape((rank, hidden), f32), (factor, merged))
    left = call(
        left_kernel,
        shape((width, 3 * rank), bf16),
        (factor,),
        scratch_shapes=[pltpu.VMEM((rank, width), f32)],
    )
    shard = width // replicas
    mine = lax.dynamic_slice_in_dim(left, lax.axis_index(DP) * shard, shard, 0)
    select = call(
        lambda *refs: select_kernel(experts, capacity, *refs),
        shape((2 * row_count, slots), bf16),
        (routes_t,),
    )
    steps = [(axis, step) for axis in DP[::-1] for step in partners(lax.axis_size(axis))]
    for i, (axis, step) in enumerate(steps):
        other = from_partner(right, axis, step)
        if i == len(steps) - 4:
            other, select = lax.optimization_barrier((other, select))
        if i == len(steps) - 3:
            other, left = lax.optimization_barrier((other, left))
        if i == len(steps) - 2:
            other, mine = lax.optimization_barrier((other, mine))
        right = right + other
    error_next, weight_grad = call(
        lambda *refs: finish_kernel(replicas, *refs),
        (shape((width, hidden), bf16), shape((shard, hidden), f32)),
        (right, left, mine, merged),
        room=FULL,
        in_specs=[VMEM, VMEM, VMEM, HBM],
        out_specs=[HBM, VMEM],
        scratch_shapes=[
            pltpu.VMEM((width, hidden), bf16),
            pltpu.VMEM((width, hidden), bf16),
            dma((TILES,)),
            dma((TILES,)),
        ],
    )
    grad_tokens = call(
        combine_kernel,
        shape((row_count, width), bf16),
        (select, gates, returned),
        in_specs=[VMEM, VMEM, VMEM],
        out_specs=HBM,
        scratch_shapes=[pltpu.VMEM((row_count, width), bf16), dma((TILES,))],
    )
    return grad_tokens, error_next[None, None], weight_grad[None]


def solution(mesh):
    torus = Mesh(mesh.devices.reshape(4, 8, mesh.shape["expert"]), DP_EXPERT)
    in_specs = (
        P(DP_EXPERT, None),
        P(DP_EXPERT, None),
        P(DP_EXPERT, None),
        P(DP_EXPERT, None, None),
        P("expert", DP, None),
        P(DP, "expert", None, None),
        P("expert", None, None),
    )
    out_specs = (P(DP_EXPERT, None), P(DP, "expert", None, None), P("expert", DP, None))
    return jax.shard_map(body, mesh=torus, in_specs=in_specs, out_specs=out_specs, check_vma=False)
```

```python
import jax
import jax.numpy as jnp
from jax import lax
from jax.experimental import pallas as pl
from jax.experimental.pallas import tpu as pltpu
from jax.sharding import Mesh
from jax.sharding import PartitionSpec as P

DP = ("dp_0", "dp_1")
DP_EXPERT = ("dp_0", "dp_1", "expert")

f32, bf16 = jnp.float32, jnp.bfloat16
HBM = pl.BlockSpec(memory_space=pltpu.HBM)
VMEM = pl.BlockSpec(memory_space=pltpu.VMEM)
TILES = 7
ROOM = 16_000_000
FULL = 63_400_000
LANES = 128


def nn(a, b):
    return lax.dot_general(a, b, (((1,), (0,)), ((), ())), preferred_element_type=f32)


def nt(a, b):
    return lax.dot_general(a, b, (((1,), (1,)), ((), ())), preferred_element_type=f32)


def tn(a, b):
    return lax.dot_general(a, b, (((0,), (0,)), ((), ())), preferred_element_type=f32)


def halves(x):
    high = x.astype(bf16)
    return high, (x - high.astype(f32)).astype(bf16)


def call(kernel, outs, args, room=ROOM, **more):
    return pl.pallas_call(
        kernel,
        out_shape=outs,
        compiler_params=pltpu.CompilerParams(vmem_limit_bytes=room),
        cost_estimate=pl.CostEstimate(flops=0, bytes_accessed=0, transcendentals=0),
        **more,
    )(*args)


def one_hots(routes, experts, capacity):
    rows = routes.shape[1]
    slots = experts * capacity
    before = (
        lax.broadcasted_iota(jnp.int32, (rows, rows), 0) < lax.broadcasted_iota(jnp.int32, (rows, rows), 1)
    ).astype(bf16)
    expert = lax.broadcasted_iota(jnp.int32, (experts, rows), 0)
    slot = lax.broadcasted_iota(jnp.int32, (slots, rows), 0)
    started = jnp.zeros((experts, 1), f32)
    out = []
    for k in range(2):
        chosen = routes[k : k + 1, :]
        match = (expert == chosen).astype(f32)
        earlier = nn(match.astype(bf16), before) + started
        place = jnp.sum(match * earlier, axis=0, keepdims=True).astype(jnp.int32) + chosen * capacity
        out.append((slot == place).astype(f32))
        started = started + jnp.sum(match, axis=1, keepdims=True)
    return out


def prepare_kernel(
    experts, capacity, routes_hbm, gates_hbm, tokens_hbm, grad_hbm, sent_hbm, routes, gates, tokens, grad, sent, sem
):
    width = tokens.shape[1]
    hidden = grad.shape[2]
    copies = [
        pltpu.make_async_copy(routes_hbm, routes, sem.at[0]),
        pltpu.make_async_copy(gates_hbm, gates, sem.at[1]),
        pltpu.make_async_copy(tokens_hbm, tokens, sem.at[2]),
        pltpu.make_async_copy(grad_hbm, grad, sem.at[3]),
    ]
    for copy in copies:
        copy.start()
    copies[0].wait()
    first, second = one_hots(routes[...], experts, capacity)
    copies[1].wait()
    gate = jnp.sum(first * gates[0:1, :] + second * gates[1:2, :], axis=1, keepdims=True)
    either, first, second = (first + second).astype(bf16), first.astype(bf16), second.astype(bf16)
    copies[3].wait()
    pairs = grad[...]
    grad_0, grad_1 = pairs[:, 0, :], pairs[:, 1, :]
    copies[2].wait()
    parts = 4
    step = first.shape[0] // parts
    done = []
    for i in range(parts):
        rows = slice(i * step, (i + 1) * step)
        sent[rows, :width] = (nn(either[rows], tokens[...]) * gate[rows]).astype(bf16)
        grads = nn(first[rows], grad_0) + nn(second[rows], grad_1)
        sent[rows, width:] = grads.astype(bf16)
        copy = pltpu.make_async_copy(sent.at[rows], sent_hbm.at[rows], sem.at[4 + i])
        copy.start()
        done.append(copy)
    for copy in done:
        copy.wait()


def select_kernel(experts, capacity, routes_ref, select_ref):
    rows = routes_ref.shape[1]
    for k, places in enumerate(one_hots(routes_ref[...], experts, capacity)):
        select_ref[k * rows : (k + 1) * rows, :] = places.T.astype(bf16)


def factor_kernel(
    width, arrived_ref, weight_0, weight_hbm, error_hbm, seed_ref, grad_pre_hbm, factor_ref, weight_1, error, grad_pre, sem
):
    rank = seed_ref.shape[1]
    step = width // TILES
    tiles = [slice(i * step, (i + 1) * step) for i in range(TILES)]
    fetch = pltpu.make_async_copy(weight_hbm, weight_1, sem.at[TILES])
    fetch.start()
    loads = [
        pltpu.make_async_copy(error_hbm.at[rows], error.at[rows], sem.at[i]) for i, rows in enumerate(tiles)
    ]
    for load in loads:
        load.start()
    x = arrived_ref[:, :width]
    start = 0
    for weight in (weight_0, weight_1):
        if start:
            fetch.wait()
        lanes = slice(start, start + weight.shape[1])
        pre = nn(x, weight[...])
        s = 1.0 / (1.0 + jnp.exp(-pre))
        grad = arrived_ref[:, width + lanes.start : width + lanes.stop].astype(f32)
        grad_pre[:, lanes] = (grad * (s * (1.0 + pre * (1.0 - s)))).astype(bf16)
        start = lanes.stop
    store = pltpu.make_async_copy(grad_pre, grad_pre_hbm, sem.at[TILES + 1])
    store.start()
    seed = jnp.concatenate(halves(seed_ref[...]), axis=1)
    row = nn(grad_pre[...], seed)
    part = tn(jnp.concatenate(halves(row[:, :rank] + row[:, rank:]), axis=1), x)
    factor = part[:rank] + part[rank:]
    for i, rows in enumerate(tiles):
        loads[i].wait()
        seeded = nn(error[rows, :], seed)
        total = factor[:, rows] + (seeded[:, :rank] + seeded[:, rank:]).T
        for j in range(step // LANES):
            factor_ref[:, i * (step // LANES) + j, :] = total[:, j * LANES : (j + 1) * LANES]
    store.wait()


def merge_kernel(width, arrived_ref, grad_pre_ref, error_hbm, merged_hbm, error, merged, load_sem, store_sem):
    step = width // TILES
    tiles = [slice(i * step, (i + 1) * step) for i in range(TILES)]
    loads = [
        pltpu.make_async_copy(error_hbm.at[rows], error.at[rows], load_sem.at[i])
        for i, rows in enumerate(tiles)
    ]
    for load in loads:
        load.start()
    grad_pre = grad_pre_ref[...]
    stores = []
    for i, rows in enumerate(tiles):
        product = tn(arrived_ref[:, rows], grad_pre)
        loads[i].wait()
        merged[rows, :] = (product + error[rows, :].astype(f32)).astype(bf16)
        stores.append(pltpu.make_async_copy(merged.at[rows], merged_hbm.at[rows], store_sem.at[i]))
        stores[i].start()
    for store in stores:
        store.wait()


def rows_kernel(grad_pre_ref, weight_0, weight_1, grad_rows_hbm, grad_rows, sem):
    half = weight_0.shape[1]
    parts = sem.shape[0]
    step = grad_rows.shape[0] // parts
    stores = []
    for i in range(parts):
        rows = slice(i * step, (i + 1) * step)
        part = nt(grad_pre_ref[rows, :half], weight_0[...]) + nt(grad_pre_ref[rows, half:], weight_1[...])
        grad_rows[rows, :] = part.astype(bf16)
        stores.append(pltpu.make_async_copy(grad_rows.at[rows], grad_rows_hbm.at[rows], sem.at[i]))
        stores[i].start()
    for store in stores:
        store.wait()


def sum_and_copy_kernel(parts_ref, copies_ref):
    total = jnp.sum(parts_ref[...], axis=0)
    copies_ref[...] = jnp.broadcast_to(total[None], copies_ref.shape)


def right_kernel(factor_ref, merged_hbm, right_ref, merged, sem):
    rank = factor_ref.shape[0]
    step = 2 * LANES
    loads = []
    for i in range(sem.shape[0]):
        rows = slice(i * step, (i + 1) * step)
        loads.append(pltpu.make_async_copy(merged_hbm.at[rows], merged.at[rows], sem.at[i]))
        loads[i].start()
    total = jnp.zeros(right_ref.shape, f32)
    for i, load in enumerate(loads):
        pair = jnp.concatenate([factor_ref[:, 2 * i, :], factor_ref[:, 2 * i + 1, :]], axis=1)
        both = jnp.concatenate(halves(pair), axis=0)
        load.wait()
        part = nn(both, merged[i * step : (i + 1) * step, :])
        total = total + part[:rank] + part[rank:]
    right_ref[...] = total


def left_kernel(factor_ref, left_ref, gathered_ref):
    rank, blocks, _ = factor_ref.shape
    for j in range(blocks):
        gathered_ref[:, j * LANES : (j + 1) * LANES] = factor_ref[:, j, :]
    high, low = halves(gathered_ref[...])
    gram = nt(high, high) + nt(high, low) + nt(low, high)
    line = lax.broadcasted_iota(jnp.int32, (rank, rank), 0)
    column = lax.broadcasted_iota(jnp.int32, (rank, rank), 1)
    both = jnp.concatenate([gram, (line == column).astype(f32)], axis=1)
    own = lax.broadcasted_iota(jnp.int32, both.shape, 0)
    for i in range(rank):
        row = both[i : i + 1, :] / both[i : i + 1, i : i + 1]
        both = jnp.where(own == i, row, both - both[:, i : i + 1] * row)
    upper, lower = halves(both[:, rank:])
    left = (nn(upper, high) + nn(upper, low) + nn(lower, high)).T
    upper, lower = halves(left)
    left_ref[...] = jnp.concatenate([upper, upper, lower], axis=1)


def finish_kernel(
    count, total_ref, left_ref, mine_ref, merged_hbm, error_hbm, weight_ref, merged, error, load_sem, store_sem
):
    step = merged.shape[0] // TILES
    tiles = [slice(i * step, (i + 1) * step) for i in range(TILES)]
    loads = [
        pltpu.make_async_copy(merged_hbm.at[rows], merged.at[rows], load_sem.at[i])
        for i, rows in enumerate(tiles)
    ]
    for load in loads:
        load.start()
    high, low = halves(total_ref[...] / count)
    right = jnp.concatenate([high, low, high], axis=0)
    weight_ref[...] = nn(mine_ref[...], right)
    stores = []
    for i, rows in enumerate(tiles):
        low_rank = nn(left_ref[rows, :], right)
        loads[i].wait()
        error[rows, :] = (merged[rows, :].astype(f32) - low_rank).astype(bf16)
        stores.append(pltpu.make_async_copy(error.at[rows], error_hbm.at[rows], store_sem.at[i]))
        stores[i].start()
    for store in stores:
        store.wait()


def combine_kernel(select_ref, gates_ref, returned_ref, out_hbm, out, store_sem):
    rows, width = out.shape
    step = width // TILES
    tiles = [slice(i * step, (i + 1) * step) for i in range(TILES)]
    gates = gates_ref[...]
    stores = []
    for i, c in enumerate(tiles):
        picked = nn(select_ref[...], returned_ref[:, c])
        out[:, c] = (picked[:rows] * gates[:, 0:1] + picked[rows:] * gates[:, 1:2]).astype(bf16)
        stores.append(pltpu.make_async_copy(out.at[:, c], out_hbm.at[:, c], store_sem.at[i]))
        stores[i].start()
    for store in stores:
        store.wait()


def in_hbm(x):
    return pltpu.with_memory_space_constraint(x, pltpu.HBM)


def shape(dims, dtype):
    return jax.ShapeDtypeStruct(dims, dtype)


def partners(size):
    steps = [1 << k for k in range(size.bit_length() - 1)]
    if len(steps) > 1:
        steps[-1] = size - 1
    return steps


def from_partner(x, axis, step):
    return lax.ppermute(x, axis, [(i, i ^ step) for i in range(lax.axis_size(axis))])


def body(tokens, routes, gates, grad_hidden, w_in, error, q_seed):
    experts = lax.axis_size("expert")
    replicas = lax.axis_size(DP)
    row_count, width = tokens.shape
    hidden = grad_hidden.shape[2]
    rank = q_seed.shape[2]
    capacity = 4 * row_count // experts
    slots = experts * capacity
    routes_t = routes.T
    dma = pltpu.SemaphoreType.DMA

    sent = call(
        lambda *refs: prepare_kernel(experts, capacity, *refs),
        shape((slots, width + hidden), bf16),
        (routes_t, gates.T, tokens, grad_hidden),
        room=FULL,
        in_specs=[HBM, HBM, HBM, HBM],
        out_specs=HBM,
        scratch_shapes=[
            pltpu.VMEM((2, row_count), jnp.int32),
            pltpu.VMEM((2, row_count), f32),
            pltpu.VMEM((row_count, width), bf16),
            pltpu.VMEM((row_count, 2, hidden), bf16),
            pltpu.VMEM((slots, width + hidden), bf16),
            dma((8,)),
        ],
    )
    w_mine, sent = lax.optimization_barrier((w_in[0], sent))
    arrived = lax.all_to_all(
        sent.reshape(experts, capacity, width + hidden), "expert", 0, 0, tiled=True
    ).reshape(slots, width + hidden)
    weight = lax.all_gather(w_mine, DP[1], tiled=True)
    half = hidden // 2
    weight_0 = lax.all_gather(weight[:, :half], DP[0], tiled=True)
    weight_1 = lax.all_gather(weight[:, half:], DP[0], tiled=True)

    blocks = width // LANES
    stored = in_hbm(error[0, 0])
    grad_pre, factor = call(
        lambda *refs: factor_kernel(width, *refs),
        (pltpu.HBM((slots, hidden), bf16), shape((rank, blocks, LANES), f32)),
        (arrived, weight_0, in_hbm(weight_1), stored, q_seed[0]),
        in_specs=[VMEM, VMEM, HBM, HBM, VMEM],
        out_specs=[HBM, VMEM],
        scratch_shapes=[
            pltpu.VMEM((width, half), bf16),
            pltpu.VMEM((width, hidden), bf16),
            pltpu.VMEM((slots, hidden), bf16),
            dma((TILES + 2,)),
        ],
    )
    each = rank // replicas
    parts = lax.all_to_all(factor, DP, 0, 0, tiled=True)
    merged = call(
        lambda *refs: merge_kernel(width, *refs),
        pltpu.HBM((width, hidden), bf16),
        (arrived, grad_pre, stored),
        in_specs=[VMEM, VMEM, HBM],
        out_specs=HBM,
        scratch_shapes=[
            pltpu.VMEM((width, hidden), bf16),
            pltpu.VMEM((width, hidden), bf16),
            dma((TILES,)),
            dma((TILES,)),
        ],
    )
    grad_rows = call(
        rows_kernel,
        pltpu.HBM((slots, width), bf16),
        (grad_pre, weight_0, weight_1),
        in_specs=[VMEM, VMEM, VMEM],
        out_specs=HBM,
        scratch_shapes=[pltpu.VMEM((slots, width), bf16), dma((2,))],
    )
    copies = call(
        sum_and_copy_kernel,
        shape((replicas, each * blocks, LANES), f32),
        (parts.reshape(replicas, each * blocks, LANES),),
    )
    factor = lax.all_to_all(copies, DP, 0, 0, tiled=True).reshape(rank, blocks, LANES)
    factor, grad_rows, merged = lax.optimization_barrier((factor, grad_rows, merged))
    returned = lax.all_to_all(
        grad_rows.reshape(experts, capacity, width), "expert", 0, 0, tiled=True
    ).reshape(slots, width)

    merged = in_hbm(merged)
    right = call(
        right_kernel,
        shape((rank, hidden), f32),
        (factor, merged),
        in_specs=[VMEM, HBM],
        scratch_shapes=[pltpu.VMEM((width, hidden), bf16), dma((blocks // 2,))],
    )
    left = call(
        left_kernel,
        shape((width, 3 * rank), bf16),
        (factor,),
        scratch_shapes=[pltpu.VMEM((rank, width), f32)],
    )
    shard = width // replicas
    mine = lax.dynamic_slice_in_dim(left, lax.axis_index(DP) * shard, shard, 0)
    select = call(
        lambda *refs: select_kernel(experts, capacity, *refs),
        shape((2 * row_count, slots), bf16),
        (routes_t,),
    )
    steps = [(axis, step) for axis in DP[::-1] for step in partners(lax.axis_size(axis))]
    for i, (axis, step) in enumerate(steps):
        other = from_partner(right, axis, step)
        if i == len(steps) - 4:
            other, select = lax.optimization_barrier((other, select))
        if i == len(steps) - 3:
            other, left = lax.optimization_barrier((other, left))
        if i == len(steps) - 2:
            other, mine = lax.optimization_barrier((other, mine))
        right = right + other
    error_next, weight_grad = call(
        lambda *refs: finish_kernel(replicas, *refs),
        (shape((width, hidden), bf16), shape((shard, hidden), f32)),
        (right, left, mine, merged),
        room=FULL,
        in_specs=[VMEM, VMEM, VMEM, HBM],
        out_specs=[HBM, VMEM],
        scratch_shapes=[
            pltpu.VMEM((width, hidden), bf16),
            pltpu.VMEM((width, hidden), bf16),
            dma((TILES,)),
            dma((TILES,)),
        ],
    )
    grad_tokens = call(
        combine_kernel,
        shape((row_count, width), bf16),
        (select, gates, returned),
        in_specs=[VMEM, VMEM, VMEM],
        out_specs=HBM,
        scratch_shapes=[pltpu.VMEM((row_count, width), bf16), dma((TILES,))],
    )
    return grad_tokens, error_next[None, None], weight_grad[None]


def solution(mesh):
    torus = Mesh(mesh.devices.reshape(4, 8, mesh.shape["expert"]), DP_EXPERT)
    in_specs = (
        P(DP_EXPERT, None),
        P(DP_EXPERT, None),
        P(DP_EXPERT, None),
        P(DP_EXPERT, None, None),
        P("expert", DP, None),
        P(DP, "expert", None, None),
        P("expert", None, None),
    )
    out_specs = (P(DP_EXPERT, None), P(DP, "expert", None, None), P("expert", DP, None))
    return jax.shard_map(body, mesh=torus, in_specs=in_specs, out_specs=out_specs, check_vma=False)
```

```python
import jax
import jax.numpy as jnp
from jax import lax
from jax.experimental import pallas as pl
from jax.experimental.pallas import tpu as pltpu
from jax.sharding import Mesh
from jax.sharding import PartitionSpec as P

DP = ("dp_0", "dp_1", "dp_2")
DP_EXPERT = ("dp_0", "dp_1", "dp_2", "expert")

f32, bf16 = jnp.float32, jnp.bfloat16
HBM = pl.BlockSpec(memory_space=pltpu.HBM)
VMEM = pl.BlockSpec(memory_space=pltpu.VMEM)
TILES = 7
ROOM = 16_000_000
FULL = 63_400_000
LANES = 128


def nn(a, b):
    return lax.dot_general(a, b, (((1,), (0,)), ((), ())), preferred_element_type=f32)


def nt(a, b):
    return lax.dot_general(a, b, (((1,), (1,)), ((), ())), preferred_element_type=f32)


def tn(a, b):
    return lax.dot_general(a, b, (((0,), (0,)), ((), ())), preferred_element_type=f32)


def halves(x):
    high = x.astype(bf16)
    return high, (x - high.astype(f32)).astype(bf16)


def call(kernel, outs, args, room=ROOM, **more):
    return pl.pallas_call(
        kernel,
        out_shape=outs,
        compiler_params=pltpu.CompilerParams(vmem_limit_bytes=room),
        cost_estimate=pl.CostEstimate(flops=0, bytes_accessed=0, transcendentals=0),
        **more,
    )(*args)


def one_hots(routes, experts, capacity):
    rows = routes.shape[1]
    slots = experts * capacity
    before = (
        lax.broadcasted_iota(jnp.int32, (rows, rows), 0) < lax.broadcasted_iota(jnp.int32, (rows, rows), 1)
    ).astype(bf16)
    expert = lax.broadcasted_iota(jnp.int32, (experts, rows), 0)
    slot = lax.broadcasted_iota(jnp.int32, (slots, rows), 0)
    started = jnp.zeros((experts, 1), f32)
    out = []
    for k in range(2):
        chosen = routes[k : k + 1, :]
        match = (expert == chosen).astype(f32)
        earlier = nn(match.astype(bf16), before) + started
        place = jnp.sum(match * earlier, axis=0, keepdims=True).astype(jnp.int32) + chosen * capacity
        out.append((slot == place).astype(f32))
        started = started + jnp.sum(match, axis=1, keepdims=True)
    return out


def prepare_kernel(
    experts, capacity, routes_hbm, gates_hbm, tokens_hbm, grad_hbm, sent_hbm, routes, gates, tokens, grad, sent, sem
):
    width = tokens.shape[1]
    copies = [
        pltpu.make_async_copy(routes_hbm, routes, sem.at[0]),
        pltpu.make_async_copy(gates_hbm, gates, sem.at[1]),
        pltpu.make_async_copy(tokens_hbm, tokens, sem.at[2]),
        pltpu.make_async_copy(grad_hbm, grad, sem.at[3]),
    ]
    for copy in copies:
        copy.start()
    copies[0].wait()
    first, second = one_hots(routes[...], experts, capacity)
    copies[1].wait()
    gate = jnp.sum(first * gates[0:1, :] + second * gates[1:2, :], axis=1, keepdims=True)
    either, first, second = (first + second).astype(bf16), first.astype(bf16), second.astype(bf16)
    copies[2].wait()
    parts = 4
    step = first.shape[0] // parts
    done = []
    for i in range(parts):
        rows = slice(i * step, (i + 1) * step)
        sent[rows, :width] = (nn(either[rows], tokens[...]) * gate[rows]).astype(bf16)
        done.append(pltpu.make_async_copy(sent.at[rows, :width], sent_hbm.at[rows, :width], sem.at[4 + i]))
        done[i].start()
    copies[3].wait()
    pairs = grad[...]
    sent[:, width:] = (nn(first, pairs[:, 0, :]) + nn(second, pairs[:, 1, :])).astype(bf16)
    done.append(pltpu.make_async_copy(sent.at[:, width:], sent_hbm.at[:, width:], sem.at[4 + parts]))
    done[parts].start()
    for copy in done:
        copy.wait()


def select_kernel(experts, capacity, routes_ref, select_ref):
    rows = routes_ref.shape[1]
    for k, places in enumerate(one_hots(routes_ref[...], experts, capacity)):
        select_ref[k * rows : (k + 1) * rows, :] = places.T.astype(bf16)


def factor_kernel(
    width, arrived_ref, weight_0, weight_hbm, error_hbm, seed_ref, grad_pre_hbm, factor_ref, weight_1, error, grad_pre, sem
):
    rank = seed_ref.shape[1]
    step = width // TILES
    tiles = [slice(i * step, (i + 1) * step) for i in range(TILES)]
    fetch = pltpu.make_async_copy(weight_hbm, weight_1, sem.at[TILES])
    fetch.start()
    loads = [
        pltpu.make_async_copy(error_hbm.at[rows], error.at[rows], sem.at[i]) for i, rows in enumerate(tiles)
    ]
    for load in loads:
        load.start()
    x = arrived_ref[:, :width]
    start = 0
    for weight in (weight_0, weight_1):
        if start:
            fetch.wait()
        lanes = slice(start, start + weight.shape[1])
        pre = nn(x, weight[...])
        s = 1.0 / (1.0 + jnp.exp(-pre))
        grad = arrived_ref[:, width + lanes.start : width + lanes.stop].astype(f32)
        grad_pre[:, lanes] = (grad * (s * (1.0 + pre * (1.0 - s)))).astype(bf16)
        start = lanes.stop
    store = pltpu.make_async_copy(grad_pre, grad_pre_hbm, sem.at[TILES + 1])
    store.start()
    seed = jnp.concatenate(halves(seed_ref[...]), axis=1)
    row = nn(grad_pre[...], seed)
    part = tn(jnp.concatenate(halves(row[:, :rank] + row[:, rank:]), axis=1), x)
    factor = part[:rank] + part[rank:]
    for i, rows in enumerate(tiles):
        loads[i].wait()
        seeded = nn(error[rows, :], seed)
        total = factor[:, rows] + (seeded[:, :rank] + seeded[:, rank:]).T
        for j in range(step // LANES):
            factor_ref[:, i * (step // LANES) + j, :] = total[:, j * LANES : (j + 1) * LANES]
    store.wait()


def merge_kernel(width, arrived_ref, grad_pre_ref, error_hbm, merged_hbm, error, merged, load_sem, store_sem):
    step = width // TILES
    tiles = [slice(i * step, (i + 1) * step) for i in range(TILES)]
    loads = [
        pltpu.make_async_copy(error_hbm.at[rows], error.at[rows], load_sem.at[i])
        for i, rows in enumerate(tiles)
    ]
    for load in loads:
        load.start()
    grad_pre = grad_pre_ref[...]
    stores = []
    for i, rows in enumerate(tiles):
        product = tn(arrived_ref[:, rows], grad_pre)
        loads[i].wait()
        merged[rows, :] = (product + error[rows, :].astype(f32)).astype(bf16)
        stores.append(pltpu.make_async_copy(merged.at[rows], merged_hbm.at[rows], store_sem.at[i]))
        stores[i].start()
    for store in stores:
        store.wait()


def rows_kernel(grad_pre_ref, weight_0, weight_1, grad_rows_hbm, grad_rows, sem):
    half = weight_0.shape[1]
    parts = sem.shape[0]
    step = grad_rows.shape[0] // parts
    stores = []
    for i in range(parts):
        rows = slice(i * step, (i + 1) * step)
        part = nt(grad_pre_ref[rows, :half], weight_0[...]) + nt(grad_pre_ref[rows, half:], weight_1[...])
        grad_rows[rows, :] = part.astype(bf16)
        stores.append(pltpu.make_async_copy(grad_rows.at[rows], grad_rows_hbm.at[rows], sem.at[i]))
        stores[i].start()
    for store in stores:
        store.wait()


def sum_and_copy_kernel(parts_ref, copies_hbm, total, sem):
    total[...] = jnp.sum(parts_ref[...], axis=0)
    copies = [
        pltpu.make_async_copy(total, copies_hbm.at[i], sem.at[i]) for i in range(copies_hbm.shape[0])
    ]
    for copy in copies:
        copy.start()
    for copy in copies:
        copy.wait()


def right_kernel(factor_ref, merged_hbm, right_ref, merged, sem):
    rank = factor_ref.shape[0]
    step = 2 * LANES
    loads = []
    for i in range(sem.shape[0]):
        rows = slice(i * step, (i + 1) * step)
        loads.append(pltpu.make_async_copy(merged_hbm.at[rows], merged.at[rows], sem.at[i]))
        loads[i].start()
    total = jnp.zeros(right_ref.shape, f32)
    for i, load in enumerate(loads):
        pair = jnp.concatenate([factor_ref[:, 2 * i, :], factor_ref[:, 2 * i + 1, :]], axis=1)
        both = jnp.concatenate(halves(pair), axis=0)
        load.wait()
        part = nn(both, merged[i * step : (i + 1) * step, :])
        total = total + part[:rank] + part[rank:]
    right_ref[...] = total


def left_kernel(factor_ref, left_ref, gathered_ref):
    rank, blocks, _ = factor_ref.shape
    for j in range(blocks):
        gathered_ref[:, j * LANES : (j + 1) * LANES] = factor_ref[:, j, :]
    high, low = halves(gathered_ref[...])
    gram = nt(high, high) + nt(high, low) + nt(low, high)
    line = lax.broadcasted_iota(jnp.int32, (rank, rank), 0)
    column = lax.broadcasted_iota(jnp.int32, (rank, rank), 1)
    both = jnp.concatenate([gram, (line == column).astype(f32)], axis=1)
    own = lax.broadcasted_iota(jnp.int32, both.shape, 0)
    for i in range(rank):
        row = both[i : i + 1, :] / both[i : i + 1, i : i + 1]
        both = jnp.where(own == i, row, both - both[:, i : i + 1] * row)
    upper, lower = halves(both[:, rank:])
    left = (nn(upper, high) + nn(upper, low) + nn(lower, high)).T
    upper, lower = halves(left)
    left_ref[...] = jnp.concatenate([upper, upper, lower], axis=1)


def finish_kernel(
    count, total_ref, left_ref, mine_ref, merged_hbm, error_hbm, weight_ref, merged, error, load_sem, store_sem
):
    step = merged.shape[0] // TILES
    tiles = [slice(i * step, (i + 1) * step) for i in range(TILES)]
    loads = [
        pltpu.make_async_copy(merged_hbm.at[rows], merged.at[rows], load_sem.at[i])
        for i, rows in enumerate(tiles)
    ]
    for load in loads:
        load.start()
    high, low = halves(total_ref[...] / count)
    right = jnp.concatenate([high, low, high], axis=0)
    weight_ref[...] = nn(mine_ref[...], right)
    stores = []
    for i, rows in enumerate(tiles):
        low_rank = nn(left_ref[rows, :], right)
        loads[i].wait()
        error[rows, :] = (merged[rows, :].astype(f32) - low_rank).astype(bf16)
        stores.append(pltpu.make_async_copy(error.at[rows], error_hbm.at[rows], store_sem.at[i]))
        stores[i].start()
    for store in stores:
        store.wait()


def combine_kernel(select_ref, gates_ref, returned_ref, out_hbm, out, store_sem):
    rows, width = out.shape
    step = width // TILES
    tiles = [slice(i * step, (i + 1) * step) for i in range(TILES)]
    gates = gates_ref[...]
    stores = []
    for i, c in enumerate(tiles):
        picked = nn(select_ref[...], returned_ref[:, c])
        out[:, c] = (picked[:rows] * gates[:, 0:1] + picked[rows:] * gates[:, 1:2]).astype(bf16)
        stores.append(pltpu.make_async_copy(out.at[:, c], out_hbm.at[:, c], store_sem.at[i]))
        stores[i].start()
    for store in stores:
        store.wait()


def in_hbm(x):
    return pltpu.with_memory_space_constraint(x, pltpu.HBM)


def shape(dims, dtype):
    return jax.ShapeDtypeStruct(dims, dtype)


def partners(size):
    steps = [1 << k for k in range(size.bit_length() - 1)]
    if len(steps) > 1:
        steps[-1] = size - 1
    return steps


def from_partner(x, axis, step):
    return lax.ppermute(x, axis, [(i, i ^ step) for i in range(lax.axis_size(axis))])


def body(tokens, routes, gates, grad_hidden, w_in, error, q_seed):
    experts = lax.axis_size("expert")
    replicas = lax.axis_size(DP)
    row_count, width = tokens.shape
    hidden = grad_hidden.shape[2]
    rank = q_seed.shape[2]
    capacity = 4 * row_count // experts
    slots = experts * capacity
    routes_t = routes.T
    dma = pltpu.SemaphoreType.DMA

    sent = call(
        lambda *refs: prepare_kernel(experts, capacity, *refs),
        shape((slots, width + hidden), bf16),
        (routes_t, gates.T, tokens, grad_hidden),
        room=FULL,
        in_specs=[HBM, HBM, HBM, HBM],
        out_specs=HBM,
        scratch_shapes=[
            pltpu.VMEM((2, row_count), jnp.int32),
            pltpu.VMEM((2, row_count), f32),
            pltpu.VMEM((row_count, width), bf16),
            pltpu.VMEM((row_count, 2, hidden), bf16),
            pltpu.VMEM((slots, width + hidden), bf16),
            dma((9,)),
        ],
    )
    w_mine, sent = lax.optimization_barrier((w_in[0], sent))
    arrived = lax.all_to_all(
        sent.reshape(experts, capacity, width + hidden), "expert", 0, 0, tiled=True
    ).reshape(slots, width + hidden)
    weight = lax.all_gather(lax.all_gather(w_mine, DP[2], tiled=True), DP[1], tiled=True)
    half = hidden // 2
    weight_0 = lax.all_gather(weight[:, :half], DP[0], tiled=True)
    weight_1 = lax.all_gather(weight[:, half:], DP[0], tiled=True)

    blocks = width // LANES
    stored = in_hbm(error[0, 0])
    grad_pre, factor = call(
        lambda *refs: factor_kernel(width, *refs),
        (pltpu.HBM((slots, hidden), bf16), shape((rank, blocks, LANES), f32)),
        (arrived, weight_0, in_hbm(weight_1), stored, q_seed[0]),
        in_specs=[VMEM, VMEM, HBM, HBM, VMEM],
        out_specs=[HBM, VMEM],
        scratch_shapes=[
            pltpu.VMEM((width, half), bf16),
            pltpu.VMEM((width, hidden), bf16),
            pltpu.VMEM((slots, hidden), bf16),
            dma((TILES + 2,)),
        ],
    )
    each = rank // replicas
    parts = lax.all_to_all(factor, DP, 0, 0, tiled=True)
    merged = call(
        lambda *refs: merge_kernel(width, *refs),
        pltpu.HBM((width, hidden), bf16),
        (arrived, grad_pre, stored),
        in_specs=[VMEM, VMEM, HBM],
        out_specs=HBM,
        scratch_shapes=[
            pltpu.VMEM((width, hidden), bf16),
            pltpu.VMEM((width, hidden), bf16),
            dma((TILES,)),
            dma((TILES,)),
        ],
    )
    grad_rows = call(
        rows_kernel,
        pltpu.HBM((slots, width), bf16),
        (grad_pre, weight_0, weight_1),
        in_specs=[VMEM, VMEM, VMEM],
        out_specs=HBM,
        scratch_shapes=[pltpu.VMEM((slots, width), bf16), dma((2,))],
    )
    copies = call(
        sum_and_copy_kernel,
        pltpu.HBM((replicas, each * blocks, LANES), f32),
        (parts.reshape(replicas, each * blocks, LANES),),
        in_specs=[VMEM],
        out_specs=HBM,
        scratch_shapes=[pltpu.VMEM((each * blocks, LANES), f32), dma((replicas,))],
    )
    factor = lax.all_to_all(copies, DP, 0, 0, tiled=True).reshape(rank, blocks, LANES)
    factor, grad_rows, merged = lax.optimization_barrier((factor, grad_rows, merged))
    returned = lax.all_to_all(
        grad_rows.reshape(experts, capacity, width), "expert", 0, 0, tiled=True
    ).reshape(slots, width)

    merged = in_hbm(merged)
    right = call(
        right_kernel,
        shape((rank, hidden), f32),
        (factor, merged),
        in_specs=[VMEM, HBM],
        scratch_shapes=[pltpu.VMEM((width, hidden), bf16), dma((blocks // 2,))],
    )
    left = call(
        left_kernel,
        shape((width, 3 * rank), bf16),
        (factor,),
        scratch_shapes=[pltpu.VMEM((rank, width), f32)],
    )
    shard = width // replicas
    mine = lax.dynamic_slice_in_dim(left, lax.axis_index(DP) * shard, shard, 0)
    select = call(
        lambda *refs: select_kernel(experts, capacity, *refs),
        shape((2 * row_count, slots), bf16),
        (routes_t,),
    )
    steps = [(axis, step) for axis in (DP[1:], DP[0]) for step in partners(lax.axis_size(axis))]
    for i, (axis, step) in enumerate(steps):
        other = from_partner(right, axis, step)
        if i == len(steps) - 4:
            other, select = lax.optimization_barrier((other, select))
        if i == len(steps) - 3:
            other, left = lax.optimization_barrier((other, left))
        if i == len(steps) - 2:
            other, mine = lax.optimization_barrier((other, mine))
        right = right + other
    error_next, weight_grad = call(
        lambda *refs: finish_kernel(replicas, *refs),
        (shape((width, hidden), bf16), shape((shard, hidden), f32)),
        (right, left, mine, merged),
        room=FULL,
        in_specs=[VMEM, VMEM, VMEM, HBM],
        out_specs=[HBM, VMEM],
        scratch_shapes=[
            pltpu.VMEM((width, hidden), bf16),
            pltpu.VMEM((width, hidden), bf16),
            dma((TILES,)),
            dma((TILES,)),
        ],
    )
    grad_tokens = call(
        combine_kernel,
        shape((row_count, width), bf16),
        (select, gates, returned),
        in_specs=[VMEM, VMEM, VMEM],
        out_specs=HBM,
        scratch_shapes=[pltpu.VMEM((row_count, width), bf16), dma((TILES,))],
    )
    return grad_tokens, error_next[None, None], weight_grad[None]


def solution(mesh):
    torus = Mesh(mesh.devices.reshape(4, 4, 2, mesh.shape["expert"]), DP_EXPERT)
    in_specs = (
        P(DP_EXPERT, None),
        P(DP_EXPERT, None),
        P(DP_EXPERT, None),
        P(DP_EXPERT, None, None),
        P("expert", DP, None),
        P(DP, "expert", None, None),
        P("expert", None, None),
    )
    out_specs = (P(DP_EXPERT, None), P(DP, "expert", None, None), P("expert", DP, None))
    return jax.shard_map(body, mesh=torus, in_specs=in_specs, out_specs=out_specs, check_vma=False)
```

```python
import jax
import jax.numpy as jnp
from jax import lax
from jax.experimental import pallas as pl
from jax.experimental.pallas import tpu as pltpu
from jax.sharding import Mesh
from jax.sharding import PartitionSpec as P

DP = ("dp_0", "dp_1", "dp_2")
DP_EXPERT = ("dp_0", "dp_1", "dp_2", "expert")

f32, bf16 = jnp.float32, jnp.bfloat16
HBM = pl.BlockSpec(memory_space=pltpu.HBM)
VMEM = pl.BlockSpec(memory_space=pltpu.VMEM)
TILES = 7
ROOM = 16_000_000
FULL = 63_400_000
LANES = 128


def nn(a, b):
    return lax.dot_general(a, b, (((1,), (0,)), ((), ())), preferred_element_type=f32)


def nt(a, b):
    return lax.dot_general(a, b, (((1,), (1,)), ((), ())), preferred_element_type=f32)


def tn(a, b):
    return lax.dot_general(a, b, (((0,), (0,)), ((), ())), preferred_element_type=f32)


def halves(x):
    high = x.astype(bf16)
    return high, (x - high.astype(f32)).astype(bf16)


def call(kernel, outs, args, room=ROOM, **more):
    return pl.pallas_call(
        kernel,
        out_shape=outs,
        compiler_params=pltpu.CompilerParams(vmem_limit_bytes=room),
        cost_estimate=pl.CostEstimate(flops=0, bytes_accessed=0, transcendentals=0),
        **more,
    )(*args)


def one_hots(routes, experts, capacity):
    rows = routes.shape[1]
    slots = experts * capacity
    before = (
        lax.broadcasted_iota(jnp.int32, (rows, rows), 0) < lax.broadcasted_iota(jnp.int32, (rows, rows), 1)
    ).astype(bf16)
    expert = lax.broadcasted_iota(jnp.int32, (experts, rows), 0)
    slot = lax.broadcasted_iota(jnp.int32, (slots, rows), 0)
    started = jnp.zeros((experts, 1), f32)
    out = []
    for k in range(2):
        chosen = routes[k : k + 1, :]
        match = (expert == chosen).astype(f32)
        earlier = nn(match.astype(bf16), before) + started
        place = jnp.sum(match * earlier, axis=0, keepdims=True).astype(jnp.int32) + chosen * capacity
        out.append((slot == place).astype(f32))
        started = started + jnp.sum(match, axis=1, keepdims=True)
    return out


def prepare_kernel(
    experts, capacity, routes_hbm, gates_hbm, tokens_hbm, grad_hbm, sent_hbm, routes, gates, tokens, grad, sent, sem
):
    width = tokens.shape[1]
    hidden = grad.shape[2]
    copies = [
        pltpu.make_async_copy(routes_hbm, routes, sem.at[0]),
        pltpu.make_async_copy(gates_hbm, gates, sem.at[1]),
        pltpu.make_async_copy(tokens_hbm, tokens, sem.at[2]),
        pltpu.make_async_copy(grad_hbm, grad, sem.at[3]),
    ]
    for copy in copies:
        copy.start()
    copies[0].wait()
    first, second = one_hots(routes[...], experts, capacity)
    copies[1].wait()
    gate = jnp.sum(first * gates[0:1, :] + second * gates[1:2, :], axis=1, keepdims=True)
    either, first, second = (first + second).astype(bf16), first.astype(bf16), second.astype(bf16)
    copies[3].wait()
    pairs = grad[...]
    grad_0, grad_1 = pairs[:, 0, :], pairs[:, 1, :]
    copies[2].wait()
    parts = 4
    step = first.shape[0] // parts
    done = []
    for i in range(parts):
        rows = slice(i * step, (i + 1) * step)
        sent[rows, :width] = (nn(either[rows], tokens[...]) * gate[rows]).astype(bf16)
        grads = nn(first[rows], grad_0) + nn(second[rows], grad_1)
        sent[rows, width:] = grads.astype(bf16)
        copy = pltpu.make_async_copy(sent.at[rows], sent_hbm.at[rows], sem.at[4 + i])
        copy.start()
        done.append(copy)
    for copy in done:
        copy.wait()


def select_kernel(experts, capacity, routes_ref, select_ref):
    rows = routes_ref.shape[1]
    for k, places in enumerate(one_hots(routes_ref[...], experts, capacity)):
        select_ref[k * rows : (k + 1) * rows, :] = places.T.astype(bf16)


def factor_kernel(
    width, arrived_ref, weight_0, weight_hbm, error_hbm, seed_ref, grad_pre_hbm, factor_hbm, weight_1, error, grad_pre, out, sem
):
    rank = seed_ref.shape[1]
    step = width // TILES
    tiles = [slice(i * step, (i + 1) * step) for i in range(TILES)]
    fetch = pltpu.make_async_copy(weight_hbm, weight_1, sem.at[TILES])
    fetch.start()
    loads = [
        pltpu.make_async_copy(error_hbm.at[rows], error.at[rows], sem.at[i]) for i, rows in enumerate(tiles)
    ]
    for load in loads:
        load.start()
    x = arrived_ref[:, :width]
    start = 0
    for weight in (weight_0, weight_1):
        if start:
            fetch.wait()
        lanes = slice(start, start + weight.shape[1])
        pre = nn(x, weight[...])
        s = 1.0 / (1.0 + jnp.exp(-pre))
        grad = arrived_ref[:, width + lanes.start : width + lanes.stop].astype(f32)
        grad_pre[:, lanes] = (grad * (s * (1.0 + pre * (1.0 - s)))).astype(bf16)
        start = lanes.stop
    store = pltpu.make_async_copy(grad_pre, grad_pre_hbm, sem.at[TILES + 1])
    store.start()
    seed = jnp.concatenate(halves(seed_ref[...]), axis=1)
    row = nn(grad_pre[...], seed)
    part = tn(jnp.concatenate(halves(row[:, :rank] + row[:, rank:]), axis=1), x)
    factor = part[:rank] + part[rank:]
    for i, rows in enumerate(tiles):
        loads[i].wait()
        seeded = nn(error[rows, :], seed)
        total = factor[:, rows] + (seeded[:, :rank] + seeded[:, rank:]).T
        for j in range(step // LANES):
            out[:, i * (step // LANES) + j, :] = total[:, j * LANES : (j + 1) * LANES]
    send = pltpu.make_async_copy(out, factor_hbm, sem.at[TILES + 2])
    send.start()
    store.wait()
    send.wait()


def merge_kernel(width, arrived_ref, grad_pre_ref, error_hbm, merged_hbm, error, merged, load_sem, store_sem):
    step = width // TILES
    tiles = [slice(i * step, (i + 1) * step) for i in range(TILES)]
    loads = [
        pltpu.make_async_copy(error_hbm.at[rows], error.at[rows], load_sem.at[i])
        for i, rows in enumerate(tiles)
    ]
    for load in loads:
        load.start()
    grad_pre = grad_pre_ref[...]
    stores = []
    for i, rows in enumerate(tiles):
        product = tn(arrived_ref[:, rows], grad_pre)
        loads[i].wait()
        merged[rows, :] = (product + error[rows, :].astype(f32)).astype(bf16)
        stores.append(pltpu.make_async_copy(merged.at[rows], merged_hbm.at[rows], store_sem.at[i]))
        stores[i].start()
    for store in stores:
        store.wait()


def rows_kernel(grad_pre_ref, weight_0, weight_1, grad_rows_hbm, grad_rows, sem):
    half = weight_0.shape[1]
    parts = sem.shape[0]
    step = grad_rows.shape[0] // parts
    stores = []
    for i in range(parts):
        rows = slice(i * step, (i + 1) * step)
        part = nt(grad_pre_ref[rows, :half], weight_0[...]) + nt(grad_pre_ref[rows, half:], weight_1[...])
        grad_rows[rows, :] = part.astype(bf16)
        stores.append(pltpu.make_async_copy(grad_rows.at[rows], grad_rows_hbm.at[rows], sem.at[i]))
        stores[i].start()
    for store in stores:
        store.wait()


def sum_and_copy_kernel(parts_ref, copies_ref):
    total = jnp.sum(parts_ref[...], axis=0)
    copies_ref[...] = jnp.broadcast_to(total[None], copies_ref.shape)


def right_kernel(factor_ref, merged_hbm, right_ref, merged, sem):
    rank = factor_ref.shape[0]
    step = 2 * LANES
    loads = []
    for i in range(sem.shape[0]):
        rows = slice(i * step, (i + 1) * step)
        loads.append(pltpu.make_async_copy(merged_hbm.at[rows], merged.at[rows], sem.at[i]))
        loads[i].start()
    total = jnp.zeros(right_ref.shape, f32)
    for i, load in enumerate(loads):
        pair = jnp.concatenate([factor_ref[:, 2 * i, :], factor_ref[:, 2 * i + 1, :]], axis=1)
        both = jnp.concatenate(halves(pair), axis=0)
        load.wait()
        part = nn(both, merged[i * step : (i + 1) * step, :])
        total = total + part[:rank] + part[rank:]
    right_ref[...] = total


def left_kernel(factor_ref, left_ref, gathered_ref):
    rank, blocks, _ = factor_ref.shape
    for j in range(blocks):
        gathered_ref[:, j * LANES : (j + 1) * LANES] = factor_ref[:, j, :]
    high, low = halves(gathered_ref[...])
    gram = nt(high, high) + nt(high, low) + nt(low, high)
    line = lax.broadcasted_iota(jnp.int32, (rank, rank), 0)
    column = lax.broadcasted_iota(jnp.int32, (rank, rank), 1)
    both = jnp.concatenate([gram, (line == column).astype(f32)], axis=1)
    own = lax.broadcasted_iota(jnp.int32, both.shape, 0)
    for i in range(rank):
        row = both[i : i + 1, :] / both[i : i + 1, i : i + 1]
        both = jnp.where(own == i, row, both - both[:, i : i + 1] * row)
    upper, lower = halves(both[:, rank:])
    left = (nn(upper, high) + nn(upper, low) + nn(lower, high)).T
    upper, lower = halves(left)
    left_ref[...] = jnp.concatenate([upper, upper, lower], axis=1)


def finish_kernel(
    count, total_ref, left_ref, mine_ref, merged_hbm, error_hbm, weight_ref, merged, error, load_sem, store_sem
):
    step = merged.shape[0] // TILES
    tiles = [slice(i * step, (i + 1) * step) for i in range(TILES)]
    loads = [
        pltpu.make_async_copy(merged_hbm.at[rows], merged.at[rows], load_sem.at[i])
        for i, rows in enumerate(tiles)
    ]
    for load in loads:
        load.start()
    high, low = halves(total_ref[...] / count)
    right = jnp.concatenate([high, low, high], axis=0)
    weight_ref[...] = nn(mine_ref[...], right)
    stores = []
    for i, rows in enumerate(tiles):
        low_rank = nn(left_ref[rows, :], right)
        loads[i].wait()
        error[rows, :] = (merged[rows, :].astype(f32) - low_rank).astype(bf16)
        stores.append(pltpu.make_async_copy(error.at[rows], error_hbm.at[rows], store_sem.at[i]))
        stores[i].start()
    for store in stores:
        store.wait()


def combine_kernel(select_ref, gates_ref, returned_ref, out_hbm, out, store_sem):
    rows, width = out.shape
    step = width // TILES
    tiles = [slice(i * step, (i + 1) * step) for i in range(TILES)]
    gates = gates_ref[...]
    stores = []
    for i, c in enumerate(tiles):
        picked = nn(select_ref[...], returned_ref[:, c])
        out[:, c] = (picked[:rows] * gates[:, 0:1] + picked[rows:] * gates[:, 1:2]).astype(bf16)
        stores.append(pltpu.make_async_copy(out.at[:, c], out_hbm.at[:, c], store_sem.at[i]))
        stores[i].start()
    for store in stores:
        store.wait()


def in_hbm(x):
    return pltpu.with_memory_space_constraint(x, pltpu.HBM)


def shape(dims, dtype):
    return jax.ShapeDtypeStruct(dims, dtype)


def partners(size):
    steps = [1 << k for k in range(size.bit_length() - 1)]
    if len(steps) > 1:
        steps[-1] = size - 1
    return steps


def from_partner(x, axis, step):
    return lax.ppermute(x, axis, [(i, i ^ step) for i in range(lax.axis_size(axis))])


def body(tokens, routes, gates, grad_hidden, w_in, error, q_seed):
    experts = lax.axis_size("expert")
    replicas = lax.axis_size(DP)
    row_count, width = tokens.shape
    hidden = grad_hidden.shape[2]
    rank = q_seed.shape[2]
    capacity = 4 * row_count // experts
    slots = experts * capacity
    routes_t = routes.T
    dma = pltpu.SemaphoreType.DMA

    sent = call(
        lambda *refs: prepare_kernel(experts, capacity, *refs),
        shape((slots, width + hidden), bf16),
        (routes_t, gates.T, tokens, grad_hidden),
        room=FULL,
        in_specs=[HBM, HBM, HBM, HBM],
        out_specs=HBM,
        scratch_shapes=[
            pltpu.VMEM((2, row_count), jnp.int32),
            pltpu.VMEM((2, row_count), f32),
            pltpu.VMEM((row_count, width), bf16),
            pltpu.VMEM((row_count, 2, hidden), bf16),
            pltpu.VMEM((slots, width + hidden), bf16),
            dma((8,)),
        ],
    )
    w_mine, sent = lax.optimization_barrier((w_in[0], sent))
    arrived = lax.all_to_all(
        sent.reshape(experts, capacity, width + hidden), "expert", 0, 0, tiled=True
    ).reshape(slots, width + hidden)
    weight = lax.all_gather(lax.all_gather(w_mine, DP[2], tiled=True), DP[1], tiled=True)
    half = hidden // 2
    weight_0 = lax.all_gather(weight[:, :half], DP[0], tiled=True)
    weight_1 = lax.all_gather(weight[:, half:], DP[0], tiled=True)

    blocks = width // LANES
    stored = in_hbm(error[0, 0])
    grad_pre, factor = call(
        lambda *refs: factor_kernel(width, *refs),
        (pltpu.HBM((slots, hidden), bf16), pltpu.HBM((rank, blocks, LANES), f32)),
        (arrived, weight_0, in_hbm(weight_1), stored, q_seed[0]),
        in_specs=[VMEM, VMEM, HBM, HBM, VMEM],
        out_specs=[HBM, HBM],
        scratch_shapes=[
            pltpu.VMEM((width, half), bf16),
            pltpu.VMEM((width, hidden), bf16),
            pltpu.VMEM((slots, hidden), bf16),
            pltpu.VMEM((rank, blocks, LANES), f32),
            dma((TILES + 3,)),
        ],
    )
    each = rank // replicas
    parts = lax.all_to_all(factor, DP, 0, 0, tiled=True)
    merged = call(
        lambda *refs: merge_kernel(width, *refs),
        pltpu.HBM((width, hidden), bf16),
        (arrived, grad_pre, stored),
        in_specs=[VMEM, VMEM, HBM],
        out_specs=HBM,
        scratch_shapes=[
            pltpu.VMEM((width, hidden), bf16),
            pltpu.VMEM((width, hidden), bf16),
            dma((TILES,)),
            dma((TILES,)),
        ],
    )
    grad_rows = call(
        rows_kernel,
        pltpu.HBM((slots, width), bf16),
        (grad_pre, weight_0, weight_1),
        in_specs=[VMEM, VMEM, VMEM],
        out_specs=HBM,
        scratch_shapes=[pltpu.VMEM((slots, width), bf16), dma((2,))],
    )
    parts, merged = lax.optimization_barrier((parts, merged))
    copies = call(
        sum_and_copy_kernel,
        shape((replicas, each * blocks, LANES), f32),
        (parts.reshape(replicas, each * blocks, LANES),),
    )
    factor = lax.all_to_all(copies, DP, 0, 0, tiled=True).reshape(rank, blocks, LANES)
    factor, grad_rows = lax.optimization_barrier((factor, grad_rows))
    returned = lax.all_to_all(
        grad_rows.reshape(experts, capacity, width), "expert", 0, 0, tiled=True
    ).reshape(slots, width)

    merged = in_hbm(merged)
    right = call(
        right_kernel,
        shape((rank, hidden), f32),
        (factor, merged),
        in_specs=[VMEM, HBM],
        scratch_shapes=[pltpu.VMEM((width, hidden), bf16), dma((blocks // 2,))],
    )
    left = call(
        left_kernel,
        shape((width, 3 * rank), bf16),
        (factor,),
        scratch_shapes=[pltpu.VMEM((rank, width), f32)],
    )
    shard = width // replicas
    mine = lax.dynamic_slice_in_dim(left, lax.axis_index(DP) * shard, shard, 0)
    select = call(
        lambda *refs: select_kernel(experts, capacity, *refs),
        shape((2 * row_count, slots), bf16),
        (routes_t,),
    )
    steps = [(axis, step) for axis in (DP[1:], DP[0]) for step in partners(lax.axis_size(axis))]
    for i, (axis, step) in enumerate(steps):
        other = from_partner(right, axis, step)
        if i == len(steps) - 4:
            other, select = lax.optimization_barrier((other, select))
        if i == len(steps) - 3:
            other, left = lax.optimization_barrier((other, left))
        if i == len(steps) - 2:
            other, mine = lax.optimization_barrier((other, mine))
        right = right + other
    error_next, weight_grad = call(
        lambda *refs: finish_kernel(replicas, *refs),
        (shape((width, hidden), bf16), shape((shard, hidden), f32)),
        (right, left, mine, merged),
        room=FULL,
        in_specs=[VMEM, VMEM, VMEM, HBM],
        out_specs=[HBM, VMEM],
        scratch_shapes=[
            pltpu.VMEM((width, hidden), bf16),
            pltpu.VMEM((width, hidden), bf16),
            dma((TILES,)),
            dma((TILES,)),
        ],
    )
    grad_tokens = call(
        combine_kernel,
        shape((row_count, width), bf16),
        (select, gates, returned),
        in_specs=[VMEM, VMEM, VMEM],
        out_specs=HBM,
        scratch_shapes=[pltpu.VMEM((row_count, width), bf16), dma((TILES,))],
    )
    return grad_tokens, error_next[None, None], weight_grad[None]


def solution(mesh):
    torus = Mesh(mesh.devices.reshape(4, 4, 2, mesh.shape["expert"]), DP_EXPERT)
    in_specs = (
        P(DP_EXPERT, None),
        P(DP_EXPERT, None),
        P(DP_EXPERT, None),
        P(DP_EXPERT, None, None),
        P("expert", DP, None),
        P(DP, "expert", None, None),
        P("expert", None, None),
    )
    out_specs = (P(DP_EXPERT, None), P(DP, "expert", None, None), P("expert", DP, None))
    return jax.shard_map(body, mesh=torus, in_specs=in_specs, out_specs=out_specs, check_vma=False)
```

```python
import jax
import jax.numpy as jnp
from jax import lax
from jax.experimental import pallas as pl
from jax.experimental.pallas import tpu as pltpu
from jax.sharding import Mesh
from jax.sharding import PartitionSpec as P

DP = ("dp_0", "dp_1", "dp_2")
DP_EXPERT = ("dp_0", "dp_1", "dp_2", "expert")

f32, bf16 = jnp.float32, jnp.bfloat16
HBM = pl.BlockSpec(memory_space=pltpu.HBM)
VMEM = pl.BlockSpec(memory_space=pltpu.VMEM)
TILES = 7
ROOM = 16_000_000
FULL = 63_400_000
LANES = 128


def nn(a, b):
    return lax.dot_general(a, b, (((1,), (0,)), ((), ())), preferred_element_type=f32)


def nt(a, b):
    return lax.dot_general(a, b, (((1,), (1,)), ((), ())), preferred_element_type=f32)


def tn(a, b):
    return lax.dot_general(a, b, (((0,), (0,)), ((), ())), preferred_element_type=f32)


def halves(x):
    high = x.astype(bf16)
    return high, (x - high.astype(f32)).astype(bf16)


def call(kernel, outs, args, room=ROOM, **more):
    return pl.pallas_call(
        kernel,
        out_shape=outs,
        compiler_params=pltpu.CompilerParams(vmem_limit_bytes=room),
        cost_estimate=pl.CostEstimate(flops=0, bytes_accessed=0, transcendentals=0),
        **more,
    )(*args)


def one_hots(routes, experts, capacity):
    rows = routes.shape[1]
    slots = experts * capacity
    before = (
        lax.broadcasted_iota(jnp.int32, (rows, rows), 0) < lax.broadcasted_iota(jnp.int32, (rows, rows), 1)
    ).astype(bf16)
    expert = lax.broadcasted_iota(jnp.int32, (experts, rows), 0)
    slot = lax.broadcasted_iota(jnp.int32, (slots, rows), 0)
    started = jnp.zeros((experts, 1), f32)
    out = []
    for k in range(2):
        chosen = routes[k : k + 1, :]
        match = (expert == chosen).astype(f32)
        earlier = nn(match.astype(bf16), before) + started
        place = jnp.sum(match * earlier, axis=0, keepdims=True).astype(jnp.int32) + chosen * capacity
        out.append((slot == place).astype(f32))
        started = started + jnp.sum(match, axis=1, keepdims=True)
    return out


def prepare_kernel(
    experts, capacity, routes_hbm, gates_hbm, tokens_hbm, grad_hbm, sent_hbm, routes, gates, tokens, grad, sent, sem
):
    width = tokens.shape[1]
    hidden = grad.shape[2]
    copies = [
        pltpu.make_async_copy(routes_hbm, routes, sem.at[0]),
        pltpu.make_async_copy(gates_hbm, gates, sem.at[1]),
        pltpu.make_async_copy(tokens_hbm, tokens, sem.at[2]),
        pltpu.make_async_copy(grad_hbm, grad, sem.at[3]),
    ]
    for copy in copies:
        copy.start()
    copies[0].wait()
    first, second = one_hots(routes[...], experts, capacity)
    copies[1].wait()
    gate = jnp.sum(first * gates[0:1, :] + second * gates[1:2, :], axis=1, keepdims=True)
    either, first, second = (first + second).astype(bf16), first.astype(bf16), second.astype(bf16)
    copies[3].wait()
    pairs = grad[...]
    grad_0, grad_1 = pairs[:, 0, :], pairs[:, 1, :]
    copies[2].wait()
    parts = 4
    step = first.shape[0] // parts
    done = []
    for i in range(parts):
        rows = slice(i * step, (i + 1) * step)
        sent[rows, :width] = (nn(either[rows], tokens[...]) * gate[rows]).astype(bf16)
        grads = nn(first[rows], grad_0) + nn(second[rows], grad_1)
        sent[rows, width:] = grads.astype(bf16)
        copy = pltpu.make_async_copy(sent.at[rows], sent_hbm.at[rows], sem.at[4 + i])
        copy.start()
        done.append(copy)
    for copy in done:
        copy.wait()


def select_kernel(experts, capacity, routes_ref, select_ref):
    rows = routes_ref.shape[1]
    for k, places in enumerate(one_hots(routes_ref[...], experts, capacity)):
        select_ref[k * rows : (k + 1) * rows, :] = places.T.astype(bf16)


def factor_kernel(
    width, arrived_ref, weight_0, weight_hbm, error_hbm, seed_ref, grad_pre_hbm, factor_ref, weight_1, error, grad_pre, sem
):
    rank = seed_ref.shape[1]
    step = width // TILES
    tiles = [slice(i * step, (i + 1) * step) for i in range(TILES)]
    fetch = pltpu.make_async_copy(weight_hbm, weight_1, sem.at[TILES])
    fetch.start()
    loads = [
        pltpu.make_async_copy(error_hbm.at[rows], error.at[rows], sem.at[i]) for i, rows in enumerate(tiles)
    ]
    for load in loads:
        load.start()
    x = arrived_ref[:, :width]
    start = 0
    for weight in (weight_0, weight_1):
        if start:
            fetch.wait()
        lanes = slice(start, start + weight.shape[1])
        pre = nn(x, weight[...])
        s = 1.0 / (1.0 + jnp.exp(-pre))
        grad = arrived_ref[:, width + lanes.start : width + lanes.stop].astype(f32)
        grad_pre[:, lanes] = (grad * (s * (1.0 + pre * (1.0 - s)))).astype(bf16)
        start = lanes.stop
    store = pltpu.make_async_copy(grad_pre, grad_pre_hbm, sem.at[TILES + 1])
    store.start()
    seed = jnp.concatenate(halves(seed_ref[...]), axis=1)
    row = nn(grad_pre[...], seed)
    part = tn(jnp.concatenate(halves(row[:, :rank] + row[:, rank:]), axis=1), x)
    factor = part[:rank] + part[rank:]
    for i, rows in enumerate(tiles):
        loads[i].wait()
        seeded = nn(error[rows, :], seed)
        total = factor[:, rows] + (seeded[:, :rank] + seeded[:, rank:]).T
        for j in range(step // LANES):
            factor_ref[:, i * (step // LANES) + j, :] = total[:, j * LANES : (j + 1) * LANES]
    store.wait()


def merge_kernel(width, arrived_ref, grad_pre_ref, error_hbm, merged_hbm, error, merged, load_sem, store_sem):
    step = width // TILES
    tiles = [slice(i * step, (i + 1) * step) for i in range(TILES)]
    loads = [
        pltpu.make_async_copy(error_hbm.at[rows], error.at[rows], load_sem.at[i])
        for i, rows in enumerate(tiles)
    ]
    for load in loads:
        load.start()
    grad_pre = grad_pre_ref[...]
    stores = []
    for i, rows in enumerate(tiles):
        product = tn(arrived_ref[:, rows], grad_pre)
        loads[i].wait()
        merged[rows, :] = (product + error[rows, :].astype(f32)).astype(bf16)
        stores.append(pltpu.make_async_copy(merged.at[rows], merged_hbm.at[rows], store_sem.at[i]))
        stores[i].start()
    for store in stores:
        store.wait()


def rows_kernel(grad_pre_ref, weight_0, weight_1, grad_rows_hbm, grad_rows, sem):
    half = weight_0.shape[1]
    parts = sem.shape[0]
    step = grad_rows.shape[0] // parts
    stores = []
    for i in range(parts):
        rows = slice(i * step, (i + 1) * step)
        part = nt(grad_pre_ref[rows, :half], weight_0[...]) + nt(grad_pre_ref[rows, half:], weight_1[...])
        grad_rows[rows, :] = part.astype(bf16)
        stores.append(pltpu.make_async_copy(grad_rows.at[rows], grad_rows_hbm.at[rows], sem.at[i]))
        stores[i].start()
    for store in stores:
        store.wait()


def sum_and_copy_kernel(parts_ref, copies_ref):
    total = jnp.sum(parts_ref[...], axis=0)
    copies_ref[...] = jnp.broadcast_to(total[None], copies_ref.shape)


def right_kernel(factor_ref, merged_hbm, right_ref, merged, sem):
    rank = factor_ref.shape[0]
    step = 2 * LANES
    loads = []
    for i in range(sem.shape[0]):
        rows = slice(i * step, (i + 1) * step)
        loads.append(pltpu.make_async_copy(merged_hbm.at[rows], merged.at[rows], sem.at[i]))
        loads[i].start()
    total = jnp.zeros(right_ref.shape, f32)
    for i, load in enumerate(loads):
        pair = jnp.concatenate([factor_ref[:, 2 * i, :], factor_ref[:, 2 * i + 1, :]], axis=1)
        both = jnp.concatenate(halves(pair), axis=0)
        load.wait()
        part = nn(both, merged[i * step : (i + 1) * step, :])
        total = total + part[:rank] + part[rank:]
    right_ref[...] = total


def left_kernel(factor_ref, left_ref, gathered_ref):
    rank, blocks, _ = factor_ref.shape
    for j in range(blocks):
        gathered_ref[:, j * LANES : (j + 1) * LANES] = factor_ref[:, j, :]
    high, low = halves(gathered_ref[...])
    gram = nt(high, high) + nt(high, low) + nt(low, high)
    line = lax.broadcasted_iota(jnp.int32, (rank, rank), 0)
    column = lax.broadcasted_iota(jnp.int32, (rank, rank), 1)
    both = jnp.concatenate([gram, (line == column).astype(f32)], axis=1)
    own = lax.broadcasted_iota(jnp.int32, both.shape, 0)
    for i in range(rank):
        row = both[i : i + 1, :] / both[i : i + 1, i : i + 1]
        both = jnp.where(own == i, row, both - both[:, i : i + 1] * row)
    upper, lower = halves(both[:, rank:])
    left = (nn(upper, high) + nn(upper, low) + nn(lower, high)).T
    upper, lower = halves(left)
    left_ref[...] = jnp.concatenate([upper, upper, lower], axis=1)


def finish_kernel(
    count, total_ref, left_ref, mine_ref, merged_hbm, error_hbm, weight_ref, merged, error, load_sem, store_sem
):
    step = merged.shape[0] // TILES
    tiles = [slice(i * step, (i + 1) * step) for i in range(TILES)]
    loads = [
        pltpu.make_async_copy(merged_hbm.at[rows], merged.at[rows], load_sem.at[i])
        for i, rows in enumerate(tiles)
    ]
    for load in loads:
        load.start()
    high, low = halves(total_ref[...] / count)
    right = jnp.concatenate([high, low, high], axis=0)
    weight_ref[...] = nn(mine_ref[...], right)
    stores = []
    for i, rows in enumerate(tiles):
        low_rank = nn(left_ref[rows, :], right)
        loads[i].wait()
        error[rows, :] = (merged[rows, :].astype(f32) - low_rank).astype(bf16)
        stores.append(pltpu.make_async_copy(error.at[rows], error_hbm.at[rows], store_sem.at[i]))
        stores[i].start()
    for store in stores:
        store.wait()


def combine_kernel(select_ref, gates_ref, returned_ref, out_hbm, out, store_sem):
    rows, width = out.shape
    step = width // TILES
    tiles = [slice(i * step, (i + 1) * step) for i in range(TILES)]
    gates = gates_ref[...]
    stores = []
    for i, c in enumerate(tiles):
        picked = nn(select_ref[...], returned_ref[:, c])
        out[:, c] = (picked[:rows] * gates[:, 0:1] + picked[rows:] * gates[:, 1:2]).astype(bf16)
        stores.append(pltpu.make_async_copy(out.at[:, c], out_hbm.at[:, c], store_sem.at[i]))
        stores[i].start()
    for store in stores:
        store.wait()


def in_hbm(x):
    return pltpu.with_memory_space_constraint(x, pltpu.HBM)


def shape(dims, dtype):
    return jax.ShapeDtypeStruct(dims, dtype)


def partners(size):
    steps = [1 << k for k in range(size.bit_length() - 1)]
    if len(steps) > 1:
        steps[-1] = size - 1
    return steps


def from_partner(x, axis, step):
    return lax.ppermute(x, axis, [(i, i ^ step) for i in range(lax.axis_size(axis))])


def body(tokens, routes, gates, grad_hidden, w_in, error, q_seed):
    experts = lax.axis_size("expert")
    replicas = lax.axis_size(DP)
    row_count, width = tokens.shape
    hidden = grad_hidden.shape[2]
    rank = q_seed.shape[2]
    capacity = 4 * row_count // experts
    slots = experts * capacity
    routes_t = routes.T
    dma = pltpu.SemaphoreType.DMA

    sent = call(
        lambda *refs: prepare_kernel(experts, capacity, *refs),
        shape((slots, width + hidden), bf16),
        (routes_t, gates.T, tokens, grad_hidden),
        room=FULL,
        in_specs=[HBM, HBM, HBM, HBM],
        out_specs=HBM,
        scratch_shapes=[
            pltpu.VMEM((2, row_count), jnp.int32),
            pltpu.VMEM((2, row_count), f32),
            pltpu.VMEM((row_count, width), bf16),
            pltpu.VMEM((row_count, 2, hidden), bf16),
            pltpu.VMEM((slots, width + hidden), bf16),
            dma((8,)),
        ],
    )
    w_mine, sent = lax.optimization_barrier((w_in[0], sent))
    arrived = lax.all_to_all(
        sent.reshape(experts, capacity, width + hidden), "expert", 0, 0, tiled=True
    ).reshape(slots, width + hidden)
    weight = lax.all_gather(lax.all_gather(w_mine, DP[2], tiled=True), DP[1], tiled=True)
    half = hidden // 2
    weight_0 = lax.all_gather(weight[:, :half], DP[0], tiled=True)
    weight_1 = lax.all_gather(weight[:, half:], DP[0], tiled=True)

    blocks = width // LANES
    stored = in_hbm(error[0, 0])
    grad_pre, factor = call(
        lambda *refs: factor_kernel(width, *refs),
        (pltpu.HBM((slots, hidden), bf16), shape((rank, blocks, LANES), f32)),
        (arrived, weight_0, in_hbm(weight_1), stored, q_seed[0]),
        in_specs=[VMEM, VMEM, HBM, HBM, VMEM],
        out_specs=[HBM, VMEM],
        scratch_shapes=[
            pltpu.VMEM((width, half), bf16),
            pltpu.VMEM((width, hidden), bf16),
            pltpu.VMEM((slots, hidden), bf16),
            dma((TILES + 2,)),
        ],
    )
    each = rank // replicas
    parts = lax.all_to_all(factor, DP, 0, 0, tiled=True)
    merged = call(
        lambda *refs: merge_kernel(width, *refs),
        pltpu.HBM((width, hidden), bf16),
        (arrived, grad_pre, stored),
        in_specs=[VMEM, VMEM, HBM],
        out_specs=HBM,
        scratch_shapes=[
            pltpu.VMEM((width, hidden), bf16),
            pltpu.VMEM((width, hidden), bf16),
            dma((TILES,)),
            dma((TILES,)),
        ],
    )
    grad_rows = call(
        rows_kernel,
        pltpu.HBM((slots, width), bf16),
        (grad_pre, weight_0, weight_1),
        in_specs=[VMEM, VMEM, VMEM],
        out_specs=HBM,
        scratch_shapes=[pltpu.VMEM((slots, width), bf16), dma((2,))],
    )
    copies = call(
        sum_and_copy_kernel,
        shape((replicas, each * blocks, LANES), f32),
        (parts.reshape(replicas, each * blocks, LANES),),
    )
    factor = lax.all_to_all(copies, DP, 0, 0, tiled=True).reshape(rank, blocks, LANES)
    factor, grad_rows, merged = lax.optimization_barrier((factor, grad_rows, merged))
    returned = lax.all_to_all(
        grad_rows.reshape(experts, capacity, width), "expert", 0, 0, tiled=True
    ).reshape(slots, width)

    merged = in_hbm(merged)
    right = call(
        right_kernel,
        shape((rank, hidden), f32),
        (factor, merged),
        in_specs=[VMEM, HBM],
        scratch_shapes=[pltpu.VMEM((width, hidden), bf16), dma((blocks // 2,))],
    )
    left = call(
        left_kernel,
        shape((width, 3 * rank), bf16),
        (factor,),
        scratch_shapes=[pltpu.VMEM((rank, width), f32)],
    )
    shard = width // replicas
    mine = lax.dynamic_slice_in_dim(left, lax.axis_index(DP) * shard, shard, 0)
    select = call(
        lambda *refs: select_kernel(experts, capacity, *refs),
        shape((2 * row_count, slots), bf16),
        (routes_t,),
    )
    steps = [(axis, step) for axis in (DP[1:], DP[0]) for step in partners(lax.axis_size(axis))]
    for i, (axis, step) in enumerate(steps):
        other = from_partner(right, axis, step)
        if i == len(steps) - 4:
            other, select = lax.optimization_barrier((other, select))
        if i == len(steps) - 3:
            other, left = lax.optimization_barrier((other, left))
        if i == len(steps) - 2:
            other, mine = lax.optimization_barrier((other, mine))
        right = right + other
    error_next, weight_grad = call(
        lambda *refs: finish_kernel(replicas, *refs),
        (shape((width, hidden), bf16), shape((shard, hidden), f32)),
        (right, left, mine, merged),
        room=FULL,
        in_specs=[VMEM, VMEM, VMEM, HBM],
        out_specs=[HBM, VMEM],
        scratch_shapes=[
            pltpu.VMEM((width, hidden), bf16),
            pltpu.VMEM((width, hidden), bf16),
            dma((TILES,)),
            dma((TILES,)),
        ],
    )
    grad_tokens = call(
        combine_kernel,
        shape((row_count, width), bf16),
        (select, gates, returned),
        in_specs=[VMEM, VMEM, VMEM],
        out_specs=HBM,
        scratch_shapes=[pltpu.VMEM((row_count, width), bf16), dma((TILES,))],
    )
    return grad_tokens, error_next[None, None], weight_grad[None]


def solution(mesh):
    torus = Mesh(mesh.devices.reshape(4, 4, 2, mesh.shape["expert"]), DP_EXPERT)
    in_specs = (
        P(DP_EXPERT, None),
        P(DP_EXPERT, None),
        P(DP_EXPERT, None),
        P(DP_EXPERT, None, None),
        P("expert", DP, None),
        P(DP, "expert", None, None),
        P("expert", None, None),
    )
    out_specs = (P(DP_EXPERT, None), P(DP, "expert", None, None), P("expert", DP, None))
    return jax.shard_map(body, mesh=torus, in_specs=in_specs, out_specs=out_specs, check_vma=False)
```
